256 devices in a mesh: tm: 2 (over x_lo), inline: 4 (over x_hi, core), xline: 32 (over y, z).
Axes of the slice: x: 4 (x_hi: 2, x_lo: 2; x = x_hi * 2 + x_lo), y: 4, z: 8, core: 2. Of those that a mesh axis runs over, the one named last changes fastest.
Arguments:
- coef_fine: bfloat16 [2, 256, 512, 4096], P(None, 'tm', 'inline', 'xline'), may hold values from -6 to 6
- coef_coarse: bfloat16 [2, 128, 256, 2048], P(None, 'tm', 'inline', 'xline'), may hold values from -6 to 6
- kept: int32 [2, 4, 32, 6], P('tm', 'inline', 'xline'), may hold values from 0 to 15, all different within a row
- tile_offsets: int32 [2, 4, 32, 3], P('tm', 'inline', 'xline'), may hold values from 0 to 16
Outputs:
- field_block: float32 [128, 256, 2048], P('tm', 'inline', 'xline')
The draws below stay inside these ranges and needn't reach their ends.
Inputs may be any that keep to these rules, and one draw needn't show every extreme that they name: The 6 wedges of one tile are distinct, and every wedge is kept by some tile.
All inputs are finite; a program needn't handle non-finite values.
Results may differ from the reference program's by a relative error of at most 0.0003.
Values sent between devices are 32-bit elements; how exact they have to be, the bound alone decides.
No kernel may reach another device: no remote copies, remote signals or barrier semaphores. Data moves between devices by JAX's collectives and lax.ppermute only.
A program may use at most 192 MiB of HBM per device.

```python
import math
import jax
import jax.numpy as jnp
from jax import lax

B = 128
NW = 16
KEEP = 6
LOW = 64
JIT = 8
RIM = 40
STRIDE = 64
NT = 128
NI = 256
NX = 2048
N_TM = 2
N_INLINE = 4
N_XLINE = 32


def with_ends(values, stream_key, low, high):
    spot = [jax.random.randint(jax.random.fold_in(stream_key, axis), (), 0, length) for axis, length in enumerate(values.shape)]
    widest = values.shape.index(max(values.shape))
    next_to = spot[:widest] + [(spot[widest] + 1) % values.shape[widest]] + spot[widest + 1:]
    return values.at[tuple(spot)].set(low).at[tuple(next_to)].set(high)


def block_scale(own_key, dims, shards, low, top_value):
    loudness = 1.0
    for position, parts in shards:
        heights = jax.random.uniform(jax.random.fold_in(jax.random.fold_in(own_key, 6), position), (parts,), jnp.float32, low / len(shards), top_value / len(shards))
        loudness = loudness * jnp.repeat(jnp.exp(heights), dims[position] // parts).reshape((-1,) + (1,) * (len(dims) - 1 - position))
    return loudness


def distinct(own_key, rows, count, top, lift):
    sequence = jax.random.permutation(jax.random.fold_in(own_key, 1), count)
    favour = sequence
    for power in range(3):
        favour = favour * favour // count
    favour = favour * lift // count
    lots = jax.random.randint(jax.random.fold_in(own_key, 2), (rows, count), 0, 4096) + favour
    holders = jax.random.permutation(jax.random.fold_in(own_key, 3), rows)[jnp.arange(count) % rows]
    lots = jnp.where(jnp.arange(rows)[:, None] == holders[None, :], 1 << 14, lots)
    score = lots * count + jnp.arange(count)
    return lax.top_k(score.astype(jnp.int32), top)[1].astype(jnp.int32)


def bell_draw(rng, shape, width, reach, shards=(), kind=jnp.bfloat16):
    gain = block_scale(rng, shape, shards, -0.22, 0.18) if shards else 1.0
    entries = jax.random.normal(rng, shape, jnp.float32) * width * gain
    return jnp.minimum(jnp.maximum(entries, -reach), reach).astype(kind)


def setup_inputs(seed: int = 0) -> dict:
    seeds = jax.random.split(jax.random.key(seed), 5)
    coef_fine = bell_draw(seeds[0], (2, B * N_TM, B * N_INLINE, B * N_XLINE), 1.0, 6.0, ((1, 2), (2, 4), (3, 32)))
    coef_coarse = bell_draw(seeds[1], (2, LOW * N_TM, LOW * N_INLINE, LOW * N_XLINE), 1.0, 6.0, ((1, 2), (2, 4), (3, 32)))
    kept = distinct(seeds[2], N_TM * N_INLINE * N_XLINE, NW, KEEP, 0).reshape((N_TM, N_INLINE, N_XLINE, KEEP))
    tile_offsets = with_ends(jax.random.randint(seeds[3], (N_TM, N_INLINE, N_XLINE, 3), 0, 2 * JIT + 1), jax.random.fold_in(seeds[3], 1), 0, 2 * JIT).astype(jnp.int32)
    return dict(coef_fine=coef_fine, coef_coarse=coef_coarse, kept=kept, tile_offsets=tile_offsets)


def signed_freq(size):
    index = jnp.arange(size)
    return jnp.where(index < size // 2, index, index - size).astype(jnp.float32)

def place_coarse(coarse, size):
    half = coarse.shape[1] // 2
    result = coarse
    for axis in (1, 2, 3):
        shape = list(result.shape)
        shape[axis] = size - 2 * half
        zeros = jnp.zeros(tuple(shape), jnp.float32)
        lower = lax.slice_in_dim(result, 0, half, axis=axis)
        upper = lax.slice_in_dim(result, half, 2 * half, axis=axis)
        result = jnp.concatenate([lower, zeros, upper], axis=axis)
    return result

def spectrum_of(fine, coarse, kept_row, size, wedges):
    freq = signed_freq(size)
    radius = jnp.sqrt(freq[:, None, None] ** 2 + freq[None, :, None] ** 2 + freq[None, None, :] ** 2)
    inner = size / 8.0
    ramp = jnp.clip((radius - inner) / inner, 0.0, 1.0)
    coarse_win = jnp.cos(0.5 * math.pi * ramp)
    fine_win = jnp.sin(0.5 * math.pi * ramp)
    theta = jnp.mod(jnp.arctan2(freq[None, :], freq[:, None]), math.pi)
    delta = math.pi / wedges
    centres = jnp.arange(wedges).astype(jnp.float32) * delta
    dist = jnp.mod(theta[None] - centres[:, None, None] + 0.5 * math.pi, math.pi) - 0.5 * math.pi
    windows = jnp.where(jnp.abs(dist) < delta, jnp.cos(0.5 * math.pi * dist / delta), 0.0)
    chosen = lax.optimization_barrier(jnp.sum((kept_row[:, None] == jnp.arange(wedges)[None, :]).astype(jnp.float32), axis=0))
    angular = jnp.einsum('w,wab->ab', chosen, windows, precision=lax.Precision.HIGHEST)
    weight = fine_win * angular[None]
    placed = place_coarse(coarse, size)
    real_part = weight * fine[0] + coarse_win * placed[0]
    imag_part = weight * fine[1] + coarse_win * placed[1]
    return (real_part, imag_part)

def taper_of(size):
    ramp_len = size // 2
    index = jnp.arange(size).astype(jnp.float32)
    rise = jnp.sin(math.pi * (index + 0.5) / (2.0 * ramp_len)) ** 2
    fall = jnp.sin(math.pi * (size - index - 0.5) / (2.0 * ramp_len)) ** 2
    profile = jnp.where(index < ramp_len, rise, jnp.where(index >= size - ramp_len, fall, 1.0))
    return profile[:, None, None] * profile[None, :, None] * profile[None, None, :]

def reference(coef_fine, coef_coarse, kept, tile_offsets):
    canvas = jnp.zeros((NT + 2 * RIM, NI + 2 * RIM, NX + 2 * RIM), jnp.float32)
    taper = taper_of(B)
    count = N_TM * N_INLINE * N_XLINE

    def one_tile(tile, canvas):
        first = (tile // (N_INLINE * N_XLINE)).astype(jnp.int32)
        second = (tile // N_XLINE % N_INLINE).astype(jnp.int32)
        third = (tile % N_XLINE).astype(jnp.int32)
        zero = jnp.zeros((), jnp.int32)
        fine = lax.dynamic_slice(coef_fine, (zero, first * B, second * B, third * B), (2, B, B, B)).astype(jnp.float32)
        coarse = lax.dynamic_slice(coef_coarse, (zero, first * LOW, second * LOW, third * LOW), (2, LOW, LOW, LOW)).astype(jnp.float32)
        kept_row = kept[first, second, third]
        offsets = tile_offsets[first, second, third].astype(jnp.int32)
        real_part, imag_part = spectrum_of(fine, coarse, kept_row, B, NW)
        values = jnp.real(jnp.fft.ifftn(real_part + 1j * imag_part, norm='ortho')).astype(jnp.float32) * taper
        start = (first * STRIDE + offsets[0], second * STRIDE + offsets[1], third * STRIDE + offsets[2])
        current = lax.dynamic_slice(canvas, start, (B, B, B))
        return lax.dynamic_update_slice(canvas, current + values, start)
    canvas = lax.fori_loop(0, count, one_tile, canvas)
    return canvas[RIM:RIM + NT, RIM:RIM + NI, RIM:RIM + NX]
```

```python
import math

import jax
import jax.numpy as jnp
import numpy as np
from jax import lax
from jax.experimental import pallas as pl
from jax.experimental.pallas import tpu as pltpu
from jax.sharding import PartitionSpec as P

B = 128
NW = 16
F32 = jnp.float32
BF16 = jnp.bfloat16
NTR = 104
VMEM = pltpu.VMEM
SMEM = pltpu.SMEM


def tables():
    f = np.where(np.arange(B) < B // 2, np.arange(B), np.arange(B) - B).astype(np.float64)
    theta = np.mod(np.arctan2(f[None, :], f[:, None]), np.pi)
    delta = np.pi / NW
    dist = np.mod(theta[None] - np.arange(NW)[:, None, None] * delta + np.pi / 2, np.pi) - np.pi / 2
    win = np.where(np.abs(dist) < delta, np.cos(0.5 * np.pi * dist / delta), 0.0)
    rows = np.concatenate([np.arange(0, 32), np.arange(96, 128)])
    radius = np.sqrt(np.arange(32.0)[:, None, None] ** 2 + f[rows][None, :, None] ** 2 + f[None, None, :] ** 2)
    ramp = np.clip((radius - 16.0) / 16.0, 0.0, 1.0)
    wf = np.where(ramp >= 1.0, 1.0, np.sin(0.5 * np.pi * ramp))
    wc = np.where(ramp >= 1.0, 0.0, np.cos(0.5 * np.pi * ramp))
    wf = wf.reshape(32, 4, 16, B).transpose(1, 0, 2, 3)
    wc = wc.reshape(32, 4, 16, B).transpose(1, 0, 2, 3)
    n = np.arange(B)
    p = np.where(n < 64, np.sin(np.pi * (n + 0.5) / B) ** 2, np.sin(np.pi * (B - n - 0.5) / B) ** 2)
    phase = 2 * np.pi * ((n[:, None] * n[None, :]) % B) / B
    c = np.cos(phase) * p[:, None] / math.sqrt(B)
    s = np.sin(phase) * p[:, None] / math.sqrt(B)
    e0 = np.stack([np.concatenate([c, -s], 1), np.concatenate([s, c], 1)])
    w2 = np.stack([np.concatenate([c, -s], 1).T, np.concatenate([s, c], 1).T])
    w1 = np.concatenate([c[:, :64], -s[:, :64]], 1)
    w1[:, 64] = c[:, 64]
    return [np.asarray(t, np.float32) for t in (win, wf, wc, e0, w2, w1)]


def split(x):
    hi = x.astype(BF16)
    return hi, (x - hi.astype(F32)).astype(BF16)


def dot(a, b):
    return lax.dot_general(a, b, (((1,), (0,)), ((), ())), preferred_element_type=F32)


def rows_of(table, offset):
    rolled = pltpu.roll(table, offset, 0)
    row = lax.broadcasted_iota(jnp.int32, (16, table.shape[1]), 0)
    shared = rolled[0:16]
    above = jnp.concatenate([rolled[104:128], jnp.where(row < offset, shared, 0.0)], axis=0)
    below = jnp.concatenate([jnp.where(row >= offset, shared, 0.0), rolled[16:40]], axis=0)
    return rolled[40:104], above, below


def transform_kernel(
    sc, fine, coarse, win, wf, wc, e0t, w2t, w1t, rim_out, rhs_out, wco_out,
    stage, xhi, xlo, pq, ang, e0, w2, wm,
):
    step = pl.program_id(0)
    o0, o1, o2, tm, odd = sc[0], sc[1], sc[2], sc[3], sc[4]

    @pl.when(step == 0)
    def _():
        total = win[sc[5]]
        for i in range(1, 6):
            total = total + win[sc[5 + i]]
        ang[...] = total
        parts = []
        for c in range(2):
            own, above, below = rows_of(e0t[c], o0)
            parts += [own, jnp.where(tm == 0, above, below)]
        hi, lo = split(jnp.concatenate(parts, axis=0))
        e0[0] = hi
        e0[1] = lo
        for c in range(2):
            hi, lo = split(pltpu.roll(w2t[c], o2 + 88, 1))
            w2[c] = jnp.concatenate([hi, lo], axis=1)
        own, above, below = rows_of(w1t[...], o1)
        mutual = jnp.where(odd == 0, above, below)
        outer = jnp.where(odd == 0, below, above)
        hi, lo = split(mutual)
        hi, lo = hi.astype(F32), lo.astype(F32)
        wm[...] = jnp.concatenate(
            [jnp.concatenate([hi, hi], axis=1), jnp.concatenate([lo, jnp.zeros_like(lo)], axis=1)], axis=0
        ).astype(BF16)
        hi, lo = split(jnp.concatenate([own, outer], axis=0))
        hi, lo = hi.astype(F32), lo.astype(F32)
        wco_out[...] = jnp.concatenate(
            [jnp.concatenate([hi, hi], axis=1), jnp.concatenate([lo, jnp.zeros_like(lo)], axis=1)], axis=0
        ).astype(BF16)

    inner = (step < 2) | ((step >= 6) & (step < 8))

    @pl.when(inner)
    def _():
        a = ang[pl.ds(pl.multiple_of(step * 16, 16), 16), :]
        row = lax.broadcasted_iota(jnp.int32, (16, B), 0)
        a = jnp.where((step == 6) & (row == 0), 1.0, a)

        def plane(k0, j0, radial, coarse_w):
            for c in range(2):
                small = coarse[c, j0].astype(F32)
                small = jnp.concatenate([small, small], axis=1)
                stage[c * B + k0] = (a * radial) * fine[c, k0].astype(F32) + coarse_w * small

        plane(0, 0, wf[0, 0], wc[0, 0])

        def low(q, _):
            radial = wf[0, q]
            coarse_w = wc[0, q]
            plane(q, q, radial, coarse_w)
            plane(B - q, 64 - q, radial, coarse_w)
            return 0

        lax.fori_loop(1, 32, low, 0)

        def high(k0, _):
            for c in range(2):
                stage[c * B + k0] = a * fine[c, k0].astype(F32)
            return 0

        lax.fori_loop(32, 97, high, 0)
        base = step * 16
        base_lo = jnp.where(step < 2, step * 16, step * 16 - 64)
        for r in range(16):
            hi, lo = split(stage[:, r, :])
            xhi[base + r] = hi
            xlo[base_lo + r] = lo

    @pl.when((step >= 2) & (step < 6))
    def _():
        def every(k0, _):
            for c in range(2):
                stage[c * B + k0] = fine[c, k0].astype(F32)
            return 0

        lax.fori_loop(0, B, every, 0)
        for r in range(16):
            xhi[step * 16 + r] = stage[:, r, :].astype(BF16)

    def along_xline(even, odd_part, j):
        for which, pair in ((0, even), (1, odd_part)):
            wide = [jnp.concatenate([g[:NTR], g[NTR:]], axis=1) for g in pair]
            hi, lo = split(jnp.concatenate(wide, axis=0))
            out = dot(hi, w2[which])
            out = out[:, :B] + out[:, B:] + dot(lo, w2[which, :, :B])
            pq[which * 64 + j] = out[:NTR]
            pq[which * 64 + j + 1] = out[NTR:]

    def first(k, kk, lo_pair):
        hi = jnp.concatenate([xhi[k], xhi[kk]], axis=1)
        out = dot(e0[0], hi) + dot(e0[1], hi)
        if lo_pair is not None:
            out = out + dot(e0[0], jnp.concatenate(lo_pair, axis=1))
        return out

    def inner_pair(j):
        out = first(j, B - j, (xlo[j], xlo[64 - j]))
        return out[:, :B] + out[:, B:], out[:, :B] - out[:, B:]

    @pl.when(step == 8)
    def _():
        out = first(0, 64, (xlo[0], jnp.zeros((256, B), BF16)))
        half = out[:, B:] * ang[64:65, :]
        even0 = out[:, :B]
        odd0 = jnp.concatenate([-half[NTR:], half[:NTR]], axis=0)
        even1, odd1 = inner_pair(1)
        along_xline((even0, even1), (odd0, odd1), 0)

        def near(i, _):
            ea, oa = inner_pair(2 * i)
            eb, ob = inner_pair(2 * i + 1)
            along_xline((ea, eb), (oa, ob), 2 * i)
            return 0

        lax.fori_loop(1, 16, near, 0)

        def outer_pair(j):
            out = first(j, B - j, None)
            a = out[:, :B] * ang[pl.ds(j, 1), :]
            b = out[:, B:] * ang[pl.ds(B - j, 1), :]
            return a + b, a - b

        def far(i, _):
            ea, oa = outer_pair(2 * i)
            eb, ob = outer_pair(2 * i + 1)
            along_xline((ea, eb), (oa, ob), 2 * i)
            return 0

        lax.fori_loop(16, 32, far, 0)
        rim_out[13 * 8 : 14 * 8] = jnp.full((8, 40, B), o2.astype(F32), F32)

    @pl.when(step >= 9)
    def _():
        n0 = (step - 9) * 8
        for pair in range(4):
            x = jnp.concatenate([pq[:, n0 + 2 * pair, :], pq[:, n0 + 2 * pair + 1, :]], axis=1)
            hi, lo = split(x)
            rhs = jnp.concatenate([hi, lo], axis=0)
            rhs_out[pair] = rhs
            out = dot(wm[...], rhs)
            out = out[:40] + out[40:]
            rim_out[n0 + 2 * pair] = out[:, :B]
            rim_out[n0 + 2 * pair + 1] = out[:, B:]


def transform(scalars, fine, coarse, tabs):
    def edge(s):
        return jnp.where(s < 2, s, jnp.clip(s - 4, 2, 3))

    whole = pl.BlockSpec(memory_space=VMEM)
    return pl.pallas_call(
        transform_kernel,
        grid=(22,),
        in_specs=[
            pl.BlockSpec(memory_space=SMEM),
            pl.BlockSpec((2, B, 16, B), lambda s: (0, 0, jnp.minimum(s, 7), 0)),
            pl.BlockSpec((2, 64, 16, 64), lambda s: (0, 0, edge(s), 0)),
            whole,
            pl.BlockSpec((1, 32, 16, B), lambda s: (edge(s), 0, 0, 0)),
            pl.BlockSpec((1, 32, 16, B), lambda s: (edge(s), 0, 0, 0)),
            whole,
            whole,
            whole,
        ],
        out_specs=[
            whole,
            pl.BlockSpec((4, 256, 256), lambda s: (jnp.maximum(s - 9, 0), 0, 0)),
            whole,
        ],
        out_shape=[
            jax.ShapeDtypeStruct((NTR + 8, 40, B), F32),
            jax.ShapeDtypeStruct((NTR // 2, 256, 256), BF16),
            jax.ShapeDtypeStruct((208, 256), BF16),
        ],
        scratch_shapes=[
            VMEM((256, 16, B), F32),
            VMEM((B, 256, B), BF16),
            VMEM((64, 256, B), BF16),
            VMEM((B, NTR, B), F32),
            VMEM((B, B), F32),
            VMEM((2, 208, 256), BF16),
            VMEM((2, 256, 256), BF16),
            VMEM((80, 256), BF16),
        ],
        compiler_params=pltpu.CompilerParams(
            dimension_semantics=("arbitrary",), vmem_limit_bytes=50 * 2**20
        ),
        cost_estimate=pl.CostEstimate(flops=2 * 10**10, bytes_accessed=30 * 10**6, transcendentals=0),
    )(scalars, fine, coarse, *tabs)


def own_rows_kernel(rhs, wco, out):
    for pair in range(4):
        x = dot(wco[...], rhs[pair])
        x = x[:NTR] + x[NTR:]
        out[2 * pair] = x[:, :B]
        out[2 * pair + 1] = x[:, B:]


def own_rows(rhs, wco):
    return pl.pallas_call(
        own_rows_kernel,
        grid=(13,),
        in_specs=[pl.BlockSpec((4, 256, 256), lambda s: (s, 0, 0)), pl.BlockSpec(memory_space=VMEM)],
        out_specs=pl.BlockSpec((8, NTR, B), lambda s: (s, 0, 0)),
        out_shape=jax.ShapeDtypeStruct((NTR, NTR, B), F32),
        compiler_params=pltpu.CompilerParams(dimension_semantics=("arbitrary",), vmem_limit_bytes=32 * 2**20),
        cost_estimate=pl.CostEstimate(flops=52 * 2 * 208 * 256 * 256, bytes_accessed=14 * 10**6, transcendentals=0),
    )(rhs, wco)


def lanes():
    return lax.broadcasted_iota(jnp.int32, (8, B), 1)


def two_sides(value, offset):
    lane = lanes()
    return jnp.where(lane < 88 + offset, value, 0.0), jnp.where(lane >= 88 + offset, value, 0.0)


def turn(value, shift):
    shift = shift % B
    return value if shift == 0 else pltpu.roll(value, shift, 1)


def pack3(pieces, start):
    lane = lanes()
    out = turn(pieces[0], -start)
    for i in range(1, len(pieces)):
        out = jnp.where(lane < 40 * i, out, turn(pieces[i], 40 * i - start))
    return out


def unpack3(packed, place, start):
    lane = lanes()
    value = turn(packed, start - 40 * place)
    return jnp.where((lane >= start) & (lane < start + 40), value, 0.0)


def merged(co, rim, t, b, sc):
    near, far = two_sides(co[t, 8 * b : 8 * b + 8, :], sc[2])
    if b < 8:
        shift = jnp.where(sc[4] == 0, 3, 0)
        place = b - shift
        valid = (place >= 0) & (place < 5)
        place = jnp.clip(place, 0, 4)
        other = rim[t, pl.ds(pl.multiple_of(place * 8, 8), 8), :]
        other = jnp.where(valid, other, 0.0)
        near2, far2 = two_sides(other, sc[11])
        near, far = near + near2, far + far2
    return near, far


def pack_many(pieces, out, start):
    for g in range(14):
        out[g] = pack3(pieces[3 * g : 3 * g + 3], start)


def pack_kernel(sc, co, rim, zhc, zlc, zho, zlo, tmsg):
    step = pl.program_id(0)
    outer_h, outer_l = [], []
    for t in range(8):
        parts = [merged(co, rim, t, b, sc) for b in range(3)]
        zhc[t] = pack3([x[0] for x in parts], 64)
        zlc[t] = pack3([x[1] for x in parts], 88)
        for b in range(8, 13):
            near, far = merged(co, rim, t, b, sc)
            outer_h.append(near)
            outer_l.append(far)
    pack_many(outer_h, zho, 64)
    pack_many(outer_l, zlo, 88)

    @pl.when(step >= 8)
    def _():
        lane = lanes()
        for t in range(8):
            extra = None
            for b in range(3, 8):
                near, far = merged(co, rim, t, b, sc)
                tmsg[t * 5 + b - 3] = jnp.where(lane < 104, near, far)
                moved = turn(far, 16 * (b - 3) - 88)
                extra = moved if extra is None else jnp.where(lane < 16 * (b - 3), extra, moved)
            tmsg[40 + t] = extra


def pack(sc, co, rim):
    return pl.pallas_call(
        pack_kernel,
        grid=(13,),
        in_specs=[
            pl.BlockSpec(memory_space=SMEM),
            pl.BlockSpec((8, NTR, B), lambda s: (s, 0, 0)),
            pl.BlockSpec((8, 40, B), lambda s: (s, 0, 0)),
        ],
        out_specs=[
            pl.BlockSpec((8, 8, B), lambda s: (s, 0, 0)),
            pl.BlockSpec((8, 8, B), lambda s: (s, 0, 0)),
            pl.BlockSpec((14, 8, B), lambda s: (s, 0, 0)),
            pl.BlockSpec((14, 8, B), lambda s: (s, 0, 0)),
            pl.BlockSpec((48, 8, B), lambda s: (jnp.maximum(s - 8, 0), 0, 0)),
        ],
        out_shape=[
            jax.ShapeDtypeStruct((NTR, 8, B), F32),
            jax.ShapeDtypeStruct((NTR, 8, B), F32),
            jax.ShapeDtypeStruct((13 * 14, 8, B), F32),
            jax.ShapeDtypeStruct((13 * 14, 8, B), F32),
            jax.ShapeDtypeStruct((5 * 48, 8, B), F32),
        ],
        compiler_params=pltpu.CompilerParams(dimension_semantics=("arbitrary",), vmem_limit_bytes=32 * 2**20),
        cost_estimate=pl.CostEstimate(flops=10**7, bytes_accessed=11 * 10**6, transcendentals=0),
    )(sc, co, rim)


def middle_kernel(sc, co, rim, zhc, zlc, zho, zlo, tmsg, own1, tmc, tmo, zh2, zl2, own2):
    step = pl.program_id(0)
    lane = lanes()

    def first_rows(t, b):
        near, _ = merged(co, rim, t, b, sc)
        if b < 3:
            low, high = unpack3(zhc[t], b, 0), unpack3(zlc[t], b, 24)
        else:
            q = t * 5 + b - 8
            low, high = unpack3(zho[q // 3], q % 3, 0), unpack3(zlo[q // 3], q % 3, 24)
        return near + low + high

    blocks = [0, 1, 2, 8, 9, 10, 11, 12]

    @pl.when(step >= 8)
    def _():
        for t in range(4):
            for i, b in enumerate(blocks):
                both = jnp.where(lane < 64, first_rows(t, b), turn(first_rows(t + 4, b), 64))
                if b < 3:
                    tmc[t * 3 + i] = both
                else:
                    tmo[t * 5 + i - 3] = both

    @pl.when(step < 8)
    def _():
        for t in range(8):
            for i, b in enumerate(blocks):
                own1[t, 8 * i : 8 * i + 8, :] = first_rows(t, b)
        place = step - jnp.where(sc[3] == 0, 3, 0)
        valid = (place >= 0) & (place < 5)
        base = jnp.clip(place, 0, 4) * 48
        ahead, behind = [], []
        for t in range(8):
            extra = tmsg[base + 40 + t]
            for b in range(3, 8):
                near, far = merged(co, rim, t, b, sc)
                main = tmsg[base + t * 5 + b - 3]
                moved = turn(extra, 88 - 16 * (b - 3))
                near = near + jnp.where(valid & (lane < 104), main, 0.0)
                far2 = jnp.where(lane >= 104, main, jnp.where(lane >= 88, moved, 0.0))
                far = far + jnp.where(valid, far2, 0.0)
                ahead.append(near)
                behind.append(far)
                own2[t, 8 * (b - 3) : 8 * (b - 3) + 8, :] = near
        pack_many(ahead, zh2, 64)
        pack_many(behind, zl2, 88)


def middle(sc, co, rim, zhc, zlc, zho, zlo, tmsg):
    def core(s):
        return (jnp.minimum(s, 7), 0, 0)

    def edge(s):
        return (jnp.maximum(s - 8, 0), 0, 0)

    def each(s):
        return (s, 0, 0)

    return pl.pallas_call(
        middle_kernel,
        grid=(13,),
        in_specs=[
            pl.BlockSpec(memory_space=SMEM),
            pl.BlockSpec((8, NTR, B), each),
            pl.BlockSpec((8, 40, B), each),
            pl.BlockSpec((8, 8, B), each),
            pl.BlockSpec((8, 8, B), each),
            pl.BlockSpec((14, 8, B), each),
            pl.BlockSpec((14, 8, B), each),
            pl.BlockSpec(memory_space=VMEM),
        ],
        out_specs=[
            pl.BlockSpec((8, 64, B), core),
            pl.BlockSpec((12, 8, B), edge),
            pl.BlockSpec((20, 8, B), edge),
            pl.BlockSpec((14, 8, B), core),
            pl.BlockSpec((14, 8, B), core),
            pl.BlockSpec((8, 40, B), core),
        ],
        out_shape=[
            jax.ShapeDtypeStruct((64, 64, B), F32),
            jax.ShapeDtypeStruct((60, 8, B), F32),
            jax.ShapeDtypeStruct((100, 8, B), F32),
            jax.ShapeDtypeStruct((8 * 14, 8, B), F32),
            jax.ShapeDtypeStruct((8 * 14, 8, B), F32),
            jax.ShapeDtypeStruct((64, 40, B), F32),
        ],
        compiler_params=pltpu.CompilerParams(dimension_semantics=("arbitrary",), vmem_limit_bytes=32 * 2**20),
        cost_estimate=pl.CostEstimate(flops=10**7, bytes_accessed=16 * 10**6, transcendentals=0),
    )(sc, co, rim, zhc, zlc, zho, zlo, tmsg)


def late_kernel(sc, own1, tmc, tmo, zh2, zl2, own2, block, dmsg):
    step = pl.program_id(0)
    lane = lanes()
    place = step - jnp.where(sc[3] == 0, 3, 0)
    valid = (place >= 0) & (place < 5)
    place = jnp.clip(place, 0, 4)

    def first_rows(t, i):
        index = place * 4 + t % 4
        both = tmc[index * 3 + i] if i < 3 else tmo[index * 5 + i - 3]
        both = both if t < 4 else turn(both, 64)
        return own1[t, 8 * i : 8 * i + 8, :] + jnp.where(valid, both, 0.0)

    for t in range(8):
        for i in range(3):
            block[t, 8 * i : 8 * i + 8, :] = first_rows(t, i)
        for i in range(5):
            q = t * 5 + i
            low, high = unpack3(zh2[q // 3], q % 3, 0), unpack3(zl2[q // 3], q % 3, 24)
            block[t, 24 + 8 * i : 32 + 8 * i, :] = own2[t, 8 * i : 8 * i + 8, :] + low + high
    for t in range(4):
        for i in range(3, 8):
            dmsg[t * 5 + i - 3] = jnp.where(lane < 64, first_rows(t, i), turn(first_rows(t + 4, i), 64))


def late(sc, own1, tmc, tmo, zh2, zl2, own2):
    def each(s):
        return (s, 0, 0)

    whole = pl.BlockSpec(memory_space=VMEM)
    return pl.pallas_call(
        late_kernel,
        grid=(8,),
        in_specs=[
            pl.BlockSpec(memory_space=SMEM),
            pl.BlockSpec((8, 64, B), each),
            whole,
            whole,
            pl.BlockSpec((14, 8, B), each),
            pl.BlockSpec((14, 8, B), each),
            pl.BlockSpec((8, 40, B), each),
        ],
        out_specs=[pl.BlockSpec((8, 64, B), each), pl.BlockSpec((20, 8, B), each)],
        out_shape=[
            jax.ShapeDtypeStruct((64, 64, B), F32),
            jax.ShapeDtypeStruct((160, 8, B), F32),
        ],
        compiler_params=pltpu.CompilerParams(dimension_semantics=("arbitrary",), vmem_limit_bytes=32 * 2**20),
        cost_estimate=pl.CostEstimate(flops=10**7, bytes_accessed=7 * 10**6, transcendentals=0),
    )(sc, own1, tmc, tmo, zh2, zl2, own2)


def last_kernel(sc, block, dmsg, out):
    shift = jnp.where(sc[4] == 0, 0, 3)
    for t in range(8):
        for b in range(8):
            place = b - shift
            valid = (place >= 0) & (place < 5)
            other = dmsg[(t % 4) * 5 + jnp.clip(place, 0, 4)]
            other = other if t < 4 else turn(other, 64)
            value = block[t, 8 * b : 8 * b + 8, :] + jnp.where(valid, other, 0.0)
            out[t, 8 * b : 8 * b + 8, :] = value[:, :64]


def last(sc, block, dmsg):
    def each(s):
        return (s, 0, 0)

    return pl.pallas_call(
        last_kernel,
        grid=(8,),
        in_specs=[
            pl.BlockSpec(memory_space=SMEM),
            pl.BlockSpec((8, 64, B), each),
            pl.BlockSpec((20, 8, B), each),
        ],
        out_specs=pl.BlockSpec((8, 64, 64), each),
        out_shape=jax.ShapeDtypeStruct((64, 64, 64), F32),
        compiler_params=pltpu.CompilerParams(dimension_semantics=("arbitrary",), vmem_limit_bytes=32 * 2**20),
        cost_estimate=pl.CostEstimate(flops=10**6, bytes_accessed=5 * 10**6, transcendentals=0),
    )(sc, block, dmsg)


def local(coef_fine, coef_coarse, kept, tile_offsets):
    tabs = [jnp.asarray(t) for t in tables()]
    n_tm, n_in, n_x = (lax.axis_size(a) for a in ("tm", "inline", "xline"))
    tm = lax.axis_index("tm").astype(jnp.int32)
    odd = (lax.axis_index("inline") % 2).astype(jnp.int32)
    sc = jnp.concatenate([tile_offsets.reshape(3), jnp.stack([tm, odd]), kept.reshape(6)])

    along = [(i, i + 1) for i in range(n_x - 1)]
    back = [(b, a) for a, b in along]
    inner = range(1, n_in - 1)
    along_o = [(i * n_x + a, i * n_x + b) for i in inner for a, b in along]
    back_o = [(b, a) for a, b in along_o]
    times = [(0, 1), (1, 0)]
    times_o = [(a * n_in + i, b * n_in + i) for i in inner for a, b in times]
    mates = [(i, i ^ 1) for i in range(n_in)]
    outer = [p for i in range(1, n_in - 1, 2) for p in ((i, i + 1), (i + 1, i))]

    rim, rhs, wco = transform(sc, coef_fine, coef_coarse, tabs)
    rim = lax.ppermute(rim, "inline", mates)
    co = own_rows(rhs, wco)
    other = rim[NTR, 0, 0].astype(jnp.int32)
    sc = jnp.concatenate([sc, other[None]])

    zhc, zlc, zho, zlo, tmsg = pack(sc, co, rim)
    tmsg = lax.ppermute(tmsg, "tm", times)
    zho = lax.ppermute(zho, ("inline", "xline"), along_o)
    zlo = lax.ppermute(zlo, ("inline", "xline"), back_o)
    zhc = lax.ppermute(zhc, "xline", along)
    zlc = lax.ppermute(zlc, "xline", back)
    own1, tmc, tmo, zh2, zl2, own2 = middle(sc, co, rim, zhc, zlc, zho, zlo, tmsg)
    tmo = lax.ppermute(tmo, ("tm", "inline"), times_o)
    tmc = lax.ppermute(tmc, "tm", times)
    zh2 = lax.ppermute(zh2, "xline", along)
    zl2 = lax.ppermute(zl2, "xline", back)
    block, dmsg = late(sc, own1, tmc, tmo, zh2, zl2, own2)
    dmsg = lax.ppermute(dmsg, "inline", outer)
    return last(sc, block, dmsg)


def solution(mesh):
    in_specs = (
        P(None, "tm", "inline", "xline"),
        P(None, "tm", "inline", "xline"),
        P("tm", "inline", "xline", None),
        P("tm", "inline", "xline", None),
    )
    out_specs = P("tm", "inline", "xline")
    return jax.shard_map(local, mesh=mesh, in_specs=in_specs, out_specs=out_specs, check_vma=False)
```

```python
import math

import jax
import jax.numpy as jnp
import numpy as np
from jax import lax
from jax.experimental import pallas as pl
from jax.experimental.pallas import tpu as pltpu
from jax.sharding import PartitionSpec as P

B = 128
NW = 16
F32 = jnp.float32
BF16 = jnp.bfloat16
NTR = 104
VMEM = pltpu.VMEM
SMEM = pltpu.SMEM


def tables():
    f = np.where(np.arange(B) < B // 2, np.arange(B), np.arange(B) - B).astype(np.float64)
    theta = np.mod(np.arctan2(f[None, :], f[:, None]), np.pi)
    delta = np.pi / NW
    dist = np.mod(theta[None] - np.arange(NW)[:, None, None] * delta + np.pi / 2, np.pi) - np.pi / 2
    win = np.where(np.abs(dist) < delta, np.cos(0.5 * np.pi * dist / delta), 0.0)
    rows = np.concatenate([np.arange(0, 32), np.arange(96, 128)])
    radius = np.sqrt(np.arange(32.0)[:, None, None] ** 2 + f[rows][None, :, None] ** 2 + f[None, None, :] ** 2)
    ramp = np.clip((radius - 16.0) / 16.0, 0.0, 1.0)
    wf = np.where(ramp >= 1.0, 1.0, np.sin(0.5 * np.pi * ramp))
    wc = np.where(ramp >= 1.0, 0.0, np.cos(0.5 * np.pi * ramp))
    wf = wf.reshape(32, 2, 32, B).transpose(1, 0, 2, 3)
    wc = wc.reshape(32, 2, 32, B).transpose(1, 0, 2, 3)
    n = np.arange(B)
    p = np.where(n < 64, np.sin(np.pi * (n + 0.5) / B) ** 2, np.sin(np.pi * (B - n - 0.5) / B) ** 2)
    phase = 2 * np.pi * ((n[:, None] * n[None, :]) % B) / B
    c = np.cos(phase) * p[:, None] / math.sqrt(B)
    s = np.sin(phase) * p[:, None] / math.sqrt(B)
    e0 = np.stack([np.concatenate([c, -s], 1), np.concatenate([s, c], 1)])
    w2 = np.stack([np.concatenate([c, -s], 1).T, np.concatenate([s, c], 1).T])
    w1 = np.concatenate([c[:, :64], -s[:, :64]], 1)
    w1[:, 64] = c[:, 64]
    return [np.asarray(t, np.float32) for t in (win, wf, wc, e0, w2, w1)]


def split(x):
    hi = x.astype(BF16)
    return hi, (x - hi.astype(F32)).astype(BF16)


def dot(a, b):
    return lax.dot_general(a, b, (((1,), (0,)), ((), ())), preferred_element_type=F32)


def rows_of(table, offset):
    rolled = pltpu.roll(table, offset, 0)
    row = lax.broadcasted_iota(jnp.int32, (16, table.shape[1]), 0)
    shared = rolled[0:16]
    above = jnp.concatenate([rolled[104:128], jnp.where(row < offset, shared, 0.0)], axis=0)
    below = jnp.concatenate([jnp.where(row >= offset, shared, 0.0), rolled[16:40]], axis=0)
    return rolled[40:104], above, below


def doubled(table):
    hi, lo = split(table)
    hi, lo = hi.astype(F32), lo.astype(F32)
    top, bottom = jnp.concatenate([hi, hi], axis=1), jnp.concatenate([lo, jnp.zeros_like(lo)], axis=1)
    return jnp.concatenate([top, bottom], axis=0).astype(BF16)


def transform_kernel(
    sc, fine, coarse, win, wf, wc, e0t, w2t, w1t, rim_out, outer_out, zho, zlo, rhs_out, wco_out,
    shi, slo, xhi, xlo, pq, ang, e0, w2, wm, gbuf,
):
    step = pl.program_id(0)
    o0, o1, o2, tm, odd = sc[0], sc[1], sc[2], sc[3], sc[4]

    @pl.when(step == 0)
    def _():
        total = win[sc[5]]
        for i in range(1, 6):
            total = total + win[sc[5 + i]]
        ang[...] = total
        parts = []
        for c in range(2):
            own, above, below = rows_of(e0t[c], o0)
            parts += [own, jnp.where(tm == 0, above, below)]
        hi, lo = split(jnp.concatenate(parts, axis=0))
        e0[:, 0:256] = hi
        e0[:, 256:512] = lo
        e0[:, 512:768] = hi
        for c in range(2):
            hi, lo = split(pltpu.roll(w2t[c], o2 + 88, 1))
            w2[c, 0:256] = jnp.concatenate([hi, lo], axis=1)
            w2[c, 256:512] = jnp.concatenate([hi, jnp.zeros_like(hi)], axis=1)
        own, above, below = rows_of(w1t[...], o1)
        mutual = jnp.where(odd == 0, above, below)
        outer = jnp.where(odd == 0, below, above)
        wm[...] = doubled(jnp.concatenate([mutual, outer], axis=0))
        wco_out[...] = doubled(own)

    @pl.when((step == 0) | (step == 3))
    def _():
        a = ang[pl.ds(pl.multiple_of(step * 32, 32), 32), :]
        row = lax.broadcasted_iota(jnp.int32, (32, B), 0)
        a = jnp.where((step == 3) & (row == 0), 1.0, a)

        def put(index, value):
            hi, lo = split(value)
            shi[index] = hi
            slo[index] = lo

        def plane(k0, j0, radial, coarse_w):
            for c in range(2):
                small = coarse[c, j0].astype(F32)
                small = jnp.concatenate([small, small], axis=1)
                put(c * B + k0, radial * fine[c, k0].astype(F32) + coarse_w * small)

        plane(0, 0, a * wf[0, 0], wc[0, 0])

        def low(q, _):
            radial = a * wf[0, q]
            coarse_w = wc[0, q]
            plane(q, q, radial, coarse_w)
            plane(B - q, 64 - q, radial, coarse_w)
            return 0

        lax.fori_loop(1, 32, low, 0, unroll=31)

        def high(i, _):
            for k0 in (32 + 2 * i, 33 + 2 * i):
                for c in range(2):
                    put(c * B + k0, a * fine[c, k0].astype(F32))
            return 0

        lax.fori_loop(0, 32, high, 0, unroll=4)
        for c in range(2):
            put(c * B + 96, a * fine[c, 96].astype(F32))
        xhi[pl.ds(step * 32, 32)] = jnp.swapaxes(shi[...], 0, 1)
        xlo[pl.ds(jnp.where(step == 0, 0, 32), 32)] = jnp.swapaxes(slo[...], 0, 1)

    @pl.when((step == 1) | (step == 2))
    def _():
        xhi[pl.ds(step * 32, 32)] = jnp.swapaxes(fine[...].reshape(256, 32, B), 0, 1)

    def along_xline(j):
        for which in range(2):
            out = dot(gbuf[which], w2[which])
            out = out[:, :B] + out[:, B:]
            pq[which * 64 + j] = out[:NTR]
            pq[which * 64 + j + 1] = out[NTR:]

    def hold(even, odd_part):
        for which, pair in ((0, even), (1, odd_part)):
            wide = [jnp.concatenate([g[:NTR], g[NTR:]], axis=1) for g in pair]
            hi, lo = split(jnp.concatenate(wide, axis=0))
            gbuf[which] = jnp.concatenate([hi, lo], axis=1)

    def first(k, kk, lo_pair):
        hi = jnp.concatenate([xhi[k], xhi[kk]], axis=1)
        if lo_pair is None:
            return dot(e0[:, 0:512], jnp.concatenate([hi, hi], axis=0))
        lo = jnp.concatenate(lo_pair, axis=1)
        return dot(e0[...], jnp.concatenate([hi, hi, lo], axis=0))

    def inner_pair(j):
        out = first(j, B - j, (xlo[j], xlo[64 - j]))
        return out[:, :B] + out[:, B:], out[:, :B] - out[:, B:]

    def outer_pair(j):
        out = first(j, B - j, None)
        a = out[:, :B] * ang[pl.ds(j, 1), :]
        b = out[:, B:] * ang[pl.ds(B - j, 1), :]
        return a + b, a - b

    @pl.when(step == 3)
    def _():
        out = first(0, 64, (xlo[0], jnp.zeros((256, B), BF16)))
        half = out[:, B:] * ang[64:65, :]
        even0 = out[:, :B]
        odd0 = jnp.concatenate([-half[NTR:], half[:NTR]], axis=0)
        even1, odd1 = inner_pair(1)
        hold((even0, even1), (odd0, odd1))

        def near(i, _):
            along_xline(2 * i - 2)
            ea, oa = inner_pair(2 * i)
            eb, ob = inner_pair(2 * i + 1)
            hold((ea, eb), (oa, ob))
            return 0

        lax.fori_loop(1, 16, near, 0, unroll=3)

        def far(i, _):
            along_xline(2 * i - 2)
            ea, oa = outer_pair(2 * i)
            eb, ob = outer_pair(2 * i + 1)
            hold((ea, eb), (oa, ob))
            return 0

        lax.fori_loop(16, 32, far, 0, unroll=2)
        along_xline(62)
        rim_out[13 * 8 : 14 * 8] = jnp.full((8, 40, B), o2.astype(F32), F32)

    @pl.when(step >= 4)
    def _():
        n0 = (step - 4) * 26
        ahead, behind = [], []
        for pair in range(13):
            x = jnp.concatenate([pq[:, n0 + 2 * pair, :], pq[:, n0 + 2 * pair + 1, :]], axis=1)
            hi, lo = split(x)
            rhs = jnp.concatenate([hi, lo], axis=0)
            rhs_out[pair] = rhs
            out = dot(wm[...], rhs)
            out = out[:80] + out[80:]
            for half in range(2):
                part = out[:, half * B : half * B + B]
                rim_out[n0 + 2 * pair + half] = part[:40]
                outer_out[2 * pair + half] = part[40:]
                for b in range(5):
                    near, far = two_sides(part[40 + 8 * b : 48 + 8 * b], o2)
                    ahead.append(near)
                    behind.append(far)
        pack_many(ahead, zho, 64)
        pack_many(behind, zlo, 88)


def transform(scalars, fine, coarse, tabs):
    def edge(s):
        return jnp.minimum(s, 1)

    def late_step(s):
        return (jnp.maximum(s - 4, 0), 0, 0)

    whole = pl.BlockSpec(memory_space=VMEM)
    return pl.pallas_call(
        transform_kernel,
        grid=(8,),
        in_specs=[
            pl.BlockSpec(memory_space=SMEM),
            pl.BlockSpec((2, B, 32, B), lambda s: (0, 0, jnp.minimum(s, 3), 0)),
            pl.BlockSpec((2, 64, 32, 64), lambda s: (0, 0, edge(s), 0)),
            whole,
            pl.BlockSpec((1, 32, 32, B), lambda s: (edge(s), 0, 0, 0)),
            pl.BlockSpec((1, 32, 32, B), lambda s: (edge(s), 0, 0, 0)),
            whole,
            whole,
            whole,
        ],
        out_specs=[
            whole,
            pl.BlockSpec((26, 40, B), late_step),
            pl.BlockSpec((44, 8, B), late_step),
            pl.BlockSpec((44, 8, B), late_step),
            pl.BlockSpec((13, 256, 256), late_step),
            whole,
        ],
        out_shape=[
            jax.ShapeDtypeStruct((NTR + 8, 40, B), F32),
            jax.ShapeDtypeStruct((NTR, 40, B), F32),
            jax.ShapeDtypeStruct((4 * 44, 8, B), F32),
            jax.ShapeDtypeStruct((4 * 44, 8, B), F32),
            jax.ShapeDtypeStruct((NTR // 2, 256, 256), BF16),
            jax.ShapeDtypeStruct((128, 256), BF16),
        ],
        scratch_shapes=[
            VMEM((256, 32, B), BF16),
            VMEM((256, 32, B), BF16),
            VMEM((B, 256, B), BF16),
            VMEM((64, 256, B), BF16),
            VMEM((B, NTR, B), F32),
            VMEM((B, B), F32),
            VMEM((208, 768), BF16),
            VMEM((2, 512, 256), BF16),
            VMEM((160, 256), BF16),
            VMEM((2, 208, 512), BF16),
        ],
        compiler_params=pltpu.CompilerParams(
            dimension_semantics=("arbitrary",), vmem_limit_bytes=63 * 2**20
        ),
        cost_estimate=pl.CostEstimate(flops=2 * 10**10, bytes_accessed=30 * 10**6, transcendentals=0),
    )(scalars, fine, coarse, *tabs)


def own_rows_kernel(rhs, wco, out):
    for pair in range(13):
        x = dot(wco[...], rhs[pair])
        x = x[:64] + x[64:]
        out[2 * pair] = x[:, :B]
        out[2 * pair + 1] = x[:, B:]


def own_rows(rhs, wco):
    return pl.pallas_call(
        own_rows_kernel,
        grid=(4,),
        in_specs=[pl.BlockSpec((13, 256, 256), lambda s: (s, 0, 0)), pl.BlockSpec(memory_space=VMEM)],
        out_specs=pl.BlockSpec((26, 64, B), lambda s: (s, 0, 0)),
        out_shape=jax.ShapeDtypeStruct((NTR, 64, B), F32),
        compiler_params=pltpu.CompilerParams(dimension_semantics=("arbitrary",), vmem_limit_bytes=63 * 2**20),
        cost_estimate=pl.CostEstimate(flops=52 * 2 * 128 * 256 * 256, bytes_accessed=11 * 10**6, transcendentals=0),
    )(rhs, wco)


def lanes():
    return lax.broadcasted_iota(jnp.int32, (8, B), 1)


def two_sides(value, offset):
    lane = lanes()
    return jnp.where(lane < 88 + offset, value, 0.0), jnp.where(lane >= 88 + offset, value, 0.0)


def turn(value, shift):
    shift = shift % B
    return value if shift == 0 else pltpu.roll(value, shift, 1)


def pack3(pieces, start):
    lane = lanes()
    out = turn(pieces[0], -start)
    for i in range(1, len(pieces)):
        out = jnp.where(lane < 40 * i, out, turn(pieces[i], 40 * i - start))
    return out


def unpack3(packed, place, start):
    lane = lanes()
    value = turn(packed, start - 40 * place)
    return jnp.where((lane >= start) & (lane < start + 40), value, 0.0)


def merged(own, rim, mate, t, b, sc):
    near, far = two_sides(own[t, 8 * b : 8 * b + 8, :], sc[2])
    place = b - jnp.where(sc[4] == 0, 3, 0)
    valid = (place >= 0) & (place < 5)
    place = jnp.clip(place, 0, 4)
    other = rim[t, pl.ds(pl.multiple_of(place * 8, 8), 8), :]
    other = jnp.where(valid, other, 0.0)
    upto = lanes().astype(F32) < 88.0 + mate[0, 0:8, :]
    return near + jnp.where(upto, other, 0.0), far + jnp.where(upto, 0.0, other)


def pack_many(pieces, out, start):
    for g in range((len(pieces) + 2) // 3):
        out[g] = pack3(pieces[3 * g : 3 * g + 3], start)


def call(kernel, grid, in_specs, outs, count, *args):
    return pl.pallas_call(
        kernel,
        grid=(grid,),
        in_specs=[pl.BlockSpec(memory_space=SMEM)] + in_specs,
        out_specs=[pl.BlockSpec(block, index) for _, block, index in outs],
        out_shape=[jax.ShapeDtypeStruct(shape, F32) for shape, _, _ in outs],
        compiler_params=pltpu.CompilerParams(dimension_semantics=("arbitrary",), vmem_limit_bytes=63 * 2**20),
        cost_estimate=pl.CostEstimate(flops=10**6, bytes_accessed=count, transcendentals=0),
    )(*args)


def each(s):
    return (s, 0, 0)


def core(s):
    return (jnp.minimum(s, 7), 0, 0)


def edge(s):
    return (jnp.maximum(s - 8, 0), 0, 0)


WHOLE = pl.BlockSpec(memory_space=VMEM)
OWN_SPECS = [
    pl.BlockSpec((8, 64, B), each),
    pl.BlockSpec((8, 40, B), each),
    pl.BlockSpec((8, 40, B), lambda s: (13, 0, 0)),
]


def pack_kernel(sc, own, rim, mate, zhc, zlc, tmsg):
    step = pl.program_id(0)
    ahead, behind = [], []
    for t in range(8):
        for b in range(5):
            near, far = merged(own, rim, mate, t, b, sc)
            ahead.append(near)
            behind.append(far)
    pack_many(ahead, zhc, 64)
    pack_many(behind, zlc, 88)

    @pl.when(step >= 8)
    def _():
        lane = lanes()
        extra = None
        for t in range(8):
            for b in range(3):
                near, far = merged(own, rim, mate, t, b + 5, sc)
                q = t * 3 + b
                tmsg[q] = jnp.where(lane < 104, near, far)
                moved = turn(far, 16 * (q % 8) - 88)
                extra = moved if q % 8 == 0 else jnp.where(lane < 16 * (q % 8), extra, moved)
                if q % 8 == 7:
                    tmsg[24 + q // 8] = extra


def pack(sc, own, rim):
    outs = [
        ((13 * 14, 8, B), (14, 8, B), each),
        ((13 * 14, 8, B), (14, 8, B), each),
        ((5 * 27, 8, B), (27, 8, B), edge),
    ]
    return call(pack_kernel, 13, OWN_SPECS, outs, 9 * 10**6, sc, own, rim, rim)


def outer_middle_kernel(sc, outer, zh, zl, own, msg):
    lane = lanes()

    def summed(t, b):
        q = lax.rem(t, 26) * 5 + b
        g, place = lax.div(t, 26) * 44 + lax.div(q, 3), lax.rem(q, 3)
        low = pltpu.roll(zh[g], lax.rem(B - 40 * place, B), 1)
        high = pltpu.roll(zl[g], lax.rem(B + 24 - 40 * place, B), 1)
        low = jnp.where(lane < 40, low, 0.0)
        high = jnp.where((lane >= 24) & (lane < 64), high, 0.0)
        return outer[t, 8 * b : 8 * b + 8, :] + low + high

    def core_rows(t, _):
        for b in range(5):
            own[t, 8 * b : 8 * b + 8, :] = summed(t, b)
        return 0

    def rim_rows(p, _):
        for b in range(5):
            even, odd = summed(64 + 2 * p, b), summed(65 + 2 * p, b)
            msg[p * 5 + b] = jnp.where(lane < 64, even, pltpu.roll(odd, 64, 1))
        return 0

    lax.fori_loop(0, 20, rim_rows, 0, unroll=2)
    lax.fori_loop(0, 64, core_rows, 0, unroll=4)


def outer_middle(sc, outer, zh, zl):
    outs = [((64, 40, B), (64, 40, B), lambda s: (0, 0, 0)), ((100, 8, B), (100, 8, B), lambda s: (0, 0, 0))]
    return call(outer_middle_kernel, 1, [WHOLE] * 3, outs, 5 * 10**6, sc, outer, zh, zl)


def middle_kernel(sc, own, rim, mate, zhc, zlc, tmsg, own1, tmc, zh2, zl2, own2):
    step = pl.program_id(0)
    lane = lanes()

    def first_rows(t, b):
        near, _ = merged(own, rim, mate, t, b, sc)
        q = t * 5 + b
        return near + unpack3(zhc[q // 3], q % 3, 0) + unpack3(zlc[q // 3], q % 3, 24)

    @pl.when(step >= 8)
    def _():
        for t in range(0, 8, 2):
            for b in range(5):
                tmc[t // 2 * 5 + b] = jnp.where(lane < 64, first_rows(t, b), turn(first_rows(t + 1, b), 64))

    @pl.when(step < 8)
    def _():
        for t in range(8):
            for b in range(5):
                own1[t, 8 * b : 8 * b + 8, :] = first_rows(t, b)
        place = step - jnp.where(sc[3] == 0, 3, 0)
        valid = (place >= 0) & (place < 5)
        base = jnp.clip(place, 0, 4) * 27
        for t in range(8):
            ahead, behind = [], []
            for b in range(3):
                q = t * 3 + b
                near, far = merged(own, rim, mate, t, b + 5, sc)
                main = tmsg[base + q]
                moved = turn(tmsg[base + 24 + q // 8], 88 - 16 * (q % 8))
                near = near + jnp.where(valid & (lane < 104), main, 0.0)
                far2 = jnp.where(lane >= 104, main, jnp.where(lane >= 88, moved, 0.0))
                far = far + jnp.where(valid, far2, 0.0)
                ahead.append(near)
                behind.append(far)
                own2[t, 8 * b : 8 * b + 8, :] = near
            zh2[t] = pack3(ahead, 64)
            zl2[t] = pack3(behind, 88)


def middle(sc, own, rim, zhc, zlc, tmsg):
    outs = [
        ((64, 40, B), (8, 40, B), core),
        ((100, 8, B), (20, 8, B), edge),
        ((64, 8, B), (8, 8, B), core),
        ((64, 8, B), (8, 8, B), core),
        ((64, 24, B), (8, 24, B), core),
    ]
    msgs = [pl.BlockSpec((14, 8, B), each), pl.BlockSpec((14, 8, B), each), WHOLE]
    return call(middle_kernel, 13, OWN_SPECS + msgs, outs, 11 * 10**6, sc, own, rim, rim, zhc, zlc, tmsg)


def time_rows(sc, own, msg, step, t, b):
    place = step - jnp.where(sc[3] == 0, 3, 0)
    valid = (place >= 0) & (place < 5)
    both = msg[(jnp.clip(place, 0, 4) * 4 + t // 2) * 5 + b]
    both = both if t % 2 == 0 else turn(both, 64)
    return own[t, 8 * b : 8 * b + 8, :] + jnp.where(valid, both, 0.0)


def outer_late_kernel(sc, own, msg, dmsg):
    step = pl.program_id(0)
    lane = lanes()
    for t in range(0, 8, 2):
        for b in range(5):
            even, odd = time_rows(sc, own, msg, step, t, b), time_rows(sc, own, msg, step, t + 1, b)
            dmsg[t // 2 * 5 + b] = jnp.where(lane < 64, even, turn(odd, 64))


def outer_late(sc, own, msg):
    outs = [((160, 8, B), (20, 8, B), each)]
    return call(outer_late_kernel, 8, [pl.BlockSpec((8, 40, B), each), WHOLE], outs, 2 * 10**6, sc, own, msg)[0]


def last_kernel(sc, own1, tmc, zh2, zl2, own2, dmsg, out):
    step = pl.program_id(0)
    shift = jnp.where(sc[4] == 0, 0, 3)
    for t in range(8):
        for b in range(8):
            if b < 5:
                value = time_rows(sc, own1, tmc, step, t, b)
            else:
                value = own2[t, 8 * (b - 5) : 8 * (b - 5) + 8, :]
                value = value + unpack3(zh2[t], b - 5, 0) + unpack3(zl2[t], b - 5, 24)
            place = b - shift
            valid = (place >= 0) & (place < 5)
            other = dmsg[t // 2 * 5 + jnp.clip(place, 0, 4)]
            other = other if t % 2 == 0 else turn(other, 64)
            value = value + jnp.where(valid, other, 0.0)
            out[t, 8 * b : 8 * b + 8, :] = value[:, :64]


def last(sc, own1, tmc, zh2, zl2, own2, dmsg):
    specs = [
        pl.BlockSpec((8, 40, B), each),
        WHOLE,
        pl.BlockSpec((8, 8, B), each),
        pl.BlockSpec((8, 8, B), each),
        pl.BlockSpec((8, 24, B), each),
        pl.BlockSpec((20, 8, B), each),
    ]
    outs = [((64, 64, 64), (8, 64, 64), each)]
    return call(last_kernel, 8, specs, outs, 7 * 10**6, sc, own1, tmc, zh2, zl2, own2, dmsg)[0]


def local(coef_fine, coef_coarse, kept, tile_offsets):
    tabs = [jnp.asarray(t) for t in tables()]
    n_tm, n_in, n_x = (lax.axis_size(a) for a in ("tm", "inline", "xline"))
    tm = lax.axis_index("tm").astype(jnp.int32)
    odd = (lax.axis_index("inline") & 1).astype(jnp.int32)
    sc = jnp.concatenate([tile_offsets.reshape(3), jnp.stack([tm, odd]), kept.reshape(6)])

    along = [(i, i + 1) for i in range(n_x - 1)]
    back = [(b, a) for a, b in along]
    inner = range(1, n_in - 1)
    along_o = [(i * n_x + a, i * n_x + b) for i in inner for a, b in along]
    back_o = [(b, a) for a, b in along_o]
    times = [(i, i ^ 1) for i in range(n_tm)]
    times_o = [(a * n_in + i, b * n_in + i) for i in inner for a, b in times]
    mates = [(i, i ^ 1) for i in range(n_in)]
    facing = [p for i in range(1, n_in - 1, 2) for p in ((i, i + 1), (i + 1, i))]

    rim, outer, zho, zlo, rhs, wco = transform(sc, coef_fine, coef_coarse, tabs)
    rim = lax.ppermute(rim, "inline", mates)
    zho = lax.ppermute(zho, ("inline", "xline"), along_o)
    zlo = lax.ppermute(zlo, ("inline", "xline"), back_o)
    own = own_rows(rhs, wco)

    zhc, zlc, tmsg = pack(sc, own, rim)
    tmsg = lax.ppermute(tmsg, "tm", times)
    zhc = lax.ppermute(zhc, "xline", along)
    zlc = lax.ppermute(zlc, "xline", back)
    outer, tmo = outer_middle(sc, outer, zho, zlo)
    tmo = lax.ppermute(tmo, ("tm", "inline"), times_o)
    own1, tmc, zh2, zl2, own2 = middle(sc, own, rim, zhc, zlc, tmsg)
    tmc = lax.ppermute(tmc, "tm", times)
    zh2 = lax.ppermute(zh2, "xline", along)
    zl2 = lax.ppermute(zl2, "xline", back)
    dmsg = outer_late(sc, outer, tmo)
    dmsg = lax.ppermute(dmsg, "inline", facing)
    return last(sc, own1, tmc, zh2, zl2, own2, dmsg)


def solution(mesh):
    in_specs = (
        P(None, "tm", "inline", "xline"),
        P(None, "tm", "inline", "xline"),
        P("tm", "inline", "xline", None),
        P("tm", "inline", "xline", None),
    )
    out_specs = P("tm", "inline", "xline")
    return jax.shard_map(local, mesh=mesh, in_specs=in_specs, out_specs=out_specs, check_vma=False)
```

```python
import math

import jax
import jax.numpy as jnp
import numpy as np
from jax import lax
from jax.experimental import pallas as pl
from jax.experimental.pallas import tpu as pltpu
from jax.sharding import PartitionSpec as P

B = 128
NW = 16
F32 = jnp.float32
BF16 = jnp.bfloat16
NTR = 104
VMEM = pltpu.VMEM
SMEM = pltpu.SMEM


def tables():
    f = np.where(np.arange(B) < B // 2, np.arange(B), np.arange(B) - B).astype(np.float64)
    theta = np.mod(np.arctan2(f[None, :], f[:, None]), np.pi)
    delta = np.pi / NW
    dist = np.mod(theta[None] - np.arange(NW)[:, None, None] * delta + np.pi / 2, np.pi) - np.pi / 2
    win = np.where(np.abs(dist) < delta, np.cos(0.5 * np.pi * dist / delta), 0.0)
    rows = np.concatenate([np.arange(0, 32), np.arange(96, 128)])
    radius = np.sqrt(np.arange(32.0)[:, None, None] ** 2 + f[rows][None, :, None] ** 2 + f[None, None, :] ** 2)
    ramp = np.clip((radius - 16.0) / 16.0, 0.0, 1.0)
    wf = np.where(ramp >= 1.0, 1.0, np.sin(0.5 * np.pi * ramp))
    wc = np.where(ramp >= 1.0, 0.0, np.cos(0.5 * np.pi * ramp))
    wf = wf.reshape(32, 2, 32, B).transpose(1, 0, 2, 3)
    wc = wc.reshape(32, 2, 32, B).transpose(1, 0, 2, 3)
    n = np.arange(B)
    p = np.where(n < 64, np.sin(np.pi * (n + 0.5) / B) ** 2, np.sin(np.pi * (B - n - 0.5) / B) ** 2)
    phase = 2 * np.pi * ((n[:, None] * n[None, :]) % B) / B
    c = np.cos(phase) * p[:, None] / math.sqrt(B)
    s = np.sin(phase) * p[:, None] / math.sqrt(B)
    e0 = np.stack([np.concatenate([c, -s], 1), np.concatenate([s, c], 1)])
    w2 = np.stack([np.concatenate([c, -s], 1).T, np.concatenate([s, c], 1).T])
    w1 = np.concatenate([c[:, :64], -s[:, :64]], 1)
    w1[:, 64] = c[:, 64]
    return [np.asarray(t, np.float32) for t in (win, wf, wc, e0, w2, w1)]


def split(x):
    hi = x.astype(BF16)
    return hi, (x - hi.astype(F32)).astype(BF16)


def dot(a, b):
    return lax.dot_general(a, b, (((1,), (0,)), ((), ())), preferred_element_type=F32)


def rows_of(table, offset):
    rolled = pltpu.roll(table, offset, 0)
    row = lax.broadcasted_iota(jnp.int32, (16, table.shape[1]), 0)
    shared = rolled[0:16]
    above = jnp.concatenate([rolled[104:128], jnp.where(row < offset, shared, 0.0)], axis=0)
    below = jnp.concatenate([jnp.where(row >= offset, shared, 0.0), rolled[16:40]], axis=0)
    return rolled[40:104], above, below


def doubled(table):
    hi, lo = split(table)
    hi, lo = hi.astype(F32), lo.astype(F32)
    top, bottom = jnp.concatenate([hi, hi], axis=1), jnp.concatenate([lo, jnp.zeros_like(lo)], axis=1)
    return jnp.concatenate([top, bottom], axis=0).astype(BF16)


def transform_kernel(
    sc, fine, coarse, win, wf, wc, e0t, w2t, w1t, rim_out, outer_out, zho, zlo, own_out,
    shi, slo, xhi, xlo, pq, ang, e0, w2, wm, gbuf,
):
    step = pl.program_id(0)
    o0, o1, o2, tm, odd = sc[0], sc[1], sc[2], sc[3], sc[4]

    @pl.when(step == 0)
    def _():
        total = win[sc[5]]
        for i in range(1, 6):
            total = total + win[sc[5 + i]]
        ang[...] = total
        parts = []
        for c in range(2):
            own, above, below = rows_of(e0t[c], o0)
            parts += [own, jnp.where(tm == 0, above, below)]
        hi, lo = split(jnp.concatenate(parts, axis=0))
        e0[:, 0:256] = hi
        e0[:, 256:512] = lo
        e0[:, 512:768] = hi
        for c in range(2):
            hi, lo = split(pltpu.roll(w2t[c], o2 + 88, 1))
            w2[c, 0:256] = jnp.concatenate([hi, lo], axis=1)
            w2[c, 256:512] = jnp.concatenate([hi, jnp.zeros_like(hi)], axis=1)
        own, above, below = rows_of(w1t[...], o1)
        mutual = jnp.where(odd == 0, above, below)
        outer = jnp.where(odd == 0, below, above)
        wm[...] = doubled(jnp.concatenate([mutual, outer, own], axis=0))

    @pl.when((step == 0) | (step == 3))
    def _():
        a = ang[pl.ds(pl.multiple_of(step * 32, 32), 32), :]
        row = lax.broadcasted_iota(jnp.int32, (32, B), 0)
        a = jnp.where((step == 3) & (row == 0), 1.0, a)

        def put(index, value):
            hi, lo = split(value)
            shi[index] = hi
            slo[index] = lo

        def plane(k0, j0, radial, coarse_w):
            for c in range(2):
                small = coarse[c, j0].astype(F32)
                small = jnp.concatenate([small, small], axis=1)
                put(c * B + k0, radial * fine[c, k0].astype(F32) + coarse_w * small)

        plane(0, 0, a * wf[0, 0], wc[0, 0])

        def low(q, _):
            radial = a * wf[0, q]
            coarse_w = wc[0, q]
            plane(q, q, radial, coarse_w)
            plane(B - q, 64 - q, radial, coarse_w)
            return 0

        lax.fori_loop(1, 32, low, 0, unroll=31)

        def high(i, _):
            for k0 in (32 + 2 * i, 33 + 2 * i):
                for c in range(2):
                    put(c * B + k0, a * fine[c, k0].astype(F32))
            return 0

        lax.fori_loop(0, 32, high, 0, unroll=4)
        for c in range(2):
            put(c * B + 96, a * fine[c, 96].astype(F32))
        xhi[pl.ds(step * 32, 32)] = jnp.swapaxes(shi[...], 0, 1)
        xlo[pl.ds(jnp.where(step == 0, 0, 32), 32)] = jnp.swapaxes(slo[...], 0, 1)

    @pl.when((step == 1) | (step == 2))
    def _():
        xhi[pl.ds(step * 32, 32)] = jnp.swapaxes(fine[...].reshape(256, 32, B), 0, 1)

    def along_xline(j):
        for which in range(2):
            out = dot(gbuf[which], w2[which])
            out = out[:, :B] + out[:, B:]
            for i in range(8):
                pq[which * 64 + j + i] = out[i * NTR : i * NTR + NTR]

    def hold(slot, even, odd_part):
        for which, pair in ((0, even), (1, odd_part)):
            wide = [jnp.concatenate([g[:NTR], g[NTR:]], axis=1) for g in pair]
            hi, lo = split(jnp.concatenate(wide, axis=0))
            gbuf[which, slot * 208 : slot * 208 + 208] = jnp.concatenate([hi, lo], axis=1)

    def first(k, kk, lo_pair):
        hi = jnp.concatenate([xhi[k], xhi[kk]], axis=1)
        if lo_pair is None:
            return dot(e0[:, 0:512], jnp.concatenate([hi, hi], axis=0))
        lo = jnp.concatenate(lo_pair, axis=1)
        return dot(e0[...], jnp.concatenate([hi, hi, lo], axis=0))

    def inner_pair(j):
        out = first(j, B - j, (xlo[j], xlo[64 - j]))
        return out[:, :B] + out[:, B:], out[:, :B] - out[:, B:]

    def outer_pair(j):
        out = first(j, B - j, None)
        a = out[:, :B] * ang[pl.ds(j, 1), :]
        b = out[:, B:] * ang[pl.ds(B - j, 1), :]
        return a + b, a - b

    @pl.when(step == 3)
    def _():
        out = first(0, 64, (xlo[0], jnp.zeros((256, B), BF16)))
        half = out[:, B:] * ang[64:65, :]
        even0 = out[:, :B]
        odd0 = jnp.concatenate([-half[NTR:], half[:NTR]], axis=0)
        even1, odd1 = inner_pair(1)
        hold(0, (even0, even1), (odd0, odd1))

        def group(pair, i, slots):
            for slot in slots:
                (ea, oa), (eb, ob) = pair(8 * i + 2 * slot), pair(8 * i + 2 * slot + 1)
                hold(slot, (ea, eb), (oa, ob))

        def eight(pair):
            def body(i, _):
                along_xline(8 * i - 8)
                group(pair, i, range(4))
                return 0

            return body

        group(inner_pair, 0, range(1, 4))
        lax.fori_loop(1, 4, eight(inner_pair), 0)
        lax.fori_loop(4, 8, eight(outer_pair), 0)
        along_xline(56)
        rim_out[13 * 8 : 14 * 8] = jnp.full((8, 40, B), o2.astype(F32), F32)

    @pl.when(step >= 4)
    def _():
        n0 = (step - 4) * 26
        ahead, behind = [], []
        for pair in range(13):
            x = jnp.concatenate([pq[:, n0 + 2 * pair, :], pq[:, n0 + 2 * pair + 1, :]], axis=1)
            hi, lo = split(x)
            rhs = jnp.concatenate([hi, lo], axis=0)
            out = dot(wm[...], rhs)
            out = out[:144] + out[144:]
            for half in range(2):
                part = out[:, half * B : half * B + B]
                rim_out[n0 + 2 * pair + half] = part[:40]
                outer_out[2 * pair + half] = part[40:80]
                own_out[2 * pair + half] = part[80:]
                for b in range(5):
                    near, far = two_sides(part[40 + 8 * b : 48 + 8 * b], o2)
                    ahead.append(near)
                    behind.append(far)
        pack_many(ahead, zho, 64)
        pack_many(behind, zlo, 88)


def transform(scalars, fine, coarse, tabs):
    def edge(s):
        return jnp.minimum(s, 1)

    def late_step(s):
        return (jnp.maximum(s - 4, 0), 0, 0)

    whole = pl.BlockSpec(memory_space=VMEM)
    return pl.pallas_call(
        transform_kernel,
        grid=(8,),
        in_specs=[
            pl.BlockSpec(memory_space=SMEM),
            pl.BlockSpec((2, B, 32, B), lambda s: (0, 0, jnp.minimum(s, 3), 0)),
            pl.BlockSpec((2, 64, 32, 64), lambda s: (0, 0, edge(s), 0)),
            whole,
            pl.BlockSpec((1, 32, 32, B), lambda s: (edge(s), 0, 0, 0)),
            pl.BlockSpec((1, 32, 32, B), lambda s: (edge(s), 0, 0, 0)),
            whole,
            whole,
            whole,
        ],
        out_specs=[
            whole,
            pl.BlockSpec((26, 40, B), late_step),
            pl.BlockSpec((44, 8, B), late_step),
            pl.BlockSpec((44, 8, B), late_step),
            pl.BlockSpec((26, 64, B), late_step),
        ],
        out_shape=[
            jax.ShapeDtypeStruct((NTR + 8, 40, B), F32),
            jax.ShapeDtypeStruct((NTR, 40, B), F32),
            jax.ShapeDtypeStruct((4 * 44, 8, B), F32),
            jax.ShapeDtypeStruct((4 * 44, 8, B), F32),
            jax.ShapeDtypeStruct((NTR, 64, B), F32),
        ],
        scratch_shapes=[
            VMEM((256, 32, B), BF16),
            VMEM((256, 32, B), BF16),
            VMEM((B, 256, B), BF16),
            VMEM((64, 256, B), BF16),
            VMEM((B, NTR, B), F32),
            VMEM((B, B), F32),
            VMEM((208, 768), BF16),
            VMEM((2, 512, 256), BF16),
            VMEM((288, 256), BF16),
            VMEM((2, 832, 512), BF16),
        ],
        compiler_params=pltpu.CompilerParams(
            dimension_semantics=("arbitrary",), vmem_limit_bytes=63 * 2**20
        ),
        cost_estimate=pl.CostEstimate(flops=2 * 10**10, bytes_accessed=30 * 10**6, transcendentals=0),
    )(scalars, fine, coarse, *tabs)


def lanes():
    return lax.broadcasted_iota(jnp.int32, (8, B), 1)


def two_sides(value, offset):
    lane = lanes()
    return jnp.where(lane < 88 + offset, value, 0.0), jnp.where(lane >= 88 + offset, value, 0.0)


def turn(value, shift):
    shift = shift % B
    return value if shift == 0 else pltpu.roll(value, shift, 1)


def pack3(pieces, start):
    lane = lanes()
    out = turn(pieces[0], -start)
    for i in range(1, len(pieces)):
        out = jnp.where(lane < 40 * i, out, turn(pieces[i], 40 * i - start))
    return out


def unpack3(packed, place, start):
    lane = lanes()
    value = turn(packed, start - 40 * place)
    return jnp.where((lane >= start) & (lane < start + 40), value, 0.0)


def merged(own, rim, mate, t, b, sc):
    near, far = two_sides(own[t, 8 * b : 8 * b + 8, :], sc[2])
    place = b - jnp.where(sc[4] == 0, 3, 0)
    valid = (place >= 0) & (place < 5)
    place = jnp.clip(place, 0, 4)
    other = rim[t, pl.ds(pl.multiple_of(place * 8, 8), 8), :]
    other = jnp.where(valid, other, 0.0)
    upto = lanes().astype(F32) < 88.0 + mate[NTR, 0:8, :]
    return near + jnp.where(upto, other, 0.0), far + jnp.where(upto, 0.0, other)


def pack_many(pieces, out, start):
    for g in range((len(pieces) + 2) // 3):
        out[g] = pack3(pieces[3 * g : 3 * g + 3], start)


def call(kernel, shapes, *args, scratch=(), weight=1000):
    return pl.pallas_call(
        kernel,
        in_specs=[pl.BlockSpec(memory_space=SMEM)] + [WHOLE] * (len(args) - 1),
        out_specs=[WHOLE] * len(shapes),
        out_shape=[jax.ShapeDtypeStruct(shape, F32) for shape in shapes],
        scratch_shapes=scratch,
        compiler_params=pltpu.CompilerParams(vmem_limit_bytes=20 * 2**20),
        cost_estimate=pl.CostEstimate(flops=1000, bytes_accessed=weight, transcendentals=0),
    )(*args)


WHOLE = pl.BlockSpec(memory_space=VMEM)


def part(ref, step, size):
    return ref.at[pl.ds(step * size, size)]


def loop(low, high, body):
    def run(i, _):
        body(i)
        return 0

    lax.fori_loop(low, high, run, 0)


def pack_time_kernel(sc, own_all, rim_all, tmsg):
    lane = lanes()

    def rims(step):
        own, rim, out = part(own_all, step, 8), part(rim_all, step, 8), part(tmsg, step - 8, 27)
        extra = None
        for t in range(8):
            for b in range(3):
                near, far = merged(own, rim, rim_all, t, b + 5, sc)
                q = t * 3 + b
                out[q] = jnp.where(lane < 104, near, far)
                moved = turn(far, 16 * (q % 8) - 88)
                extra = moved if q % 8 == 0 else jnp.where(lane < 16 * (q % 8), extra, moved)
                if q % 8 == 7:
                    out[24 + q // 8] = extra

    loop(8, 13, rims)


def pack_xline_kernel(sc, own_all, rim_all, zhc, zlc):
    def every(step):
        own, rim = part(own_all, step, 8), part(rim_all, step, 8)
        ahead, behind = [], []
        for t in range(8):
            for b in range(5):
                near, far = merged(own, rim, rim_all, t, b, sc)
                ahead.append(near)
                behind.append(far)
        pack_many(ahead, part(zhc, step, 14), 64)
        pack_many(behind, part(zlc, step, 14), 88)

    loop(0, 13, every)


def outer_middle_kernel(sc, outer_all, zho_all, zlo_all, tmo, own, held):
    lane = lanes()

    def outers(step):
        zh, zl = part(zho_all, step, 44), part(zlo_all, step, 44)
        outer, out = part(outer_all, step, 26), part(held, step, 26)
        for t in range(26):
            for b in range(5):
                q = t * 5 + b
                sides = unpack3(zh[q // 3], q % 3, 0) + unpack3(zl[q // 3], q % 3, 24)
                out[t, 8 * b : 8 * b + 8, :] = outer[t, 8 * b : 8 * b + 8, :] + sides

    def outer_rims(p):
        for b in range(5):
            rows = slice(8 * b, 8 * b + 8)
            tmo[p * 5 + b] = jnp.where(lane < 64, held[64 + 2 * p, rows, :], turn(held[65 + 2 * p, rows, :], 64))

    loop(0, 4, outers)
    loop(0, 20, outer_rims)
    own[...] = held[0:64]


def pack_time(sc, own, rim):
    return call(pack_time_kernel, [(5 * 27, 8, B)], sc, own, rim)[0]


def pack_xline(sc, own, rim):
    return call(pack_xline_kernel, [(13 * 14, 8, B), (13 * 14, 8, B)], sc, own, rim, weight=10**8)


def outer_middle(sc, outer, zho, zlo):
    scratch = [VMEM((NTR, 40, B), F32)]
    return call(outer_middle_kernel, [(100, 8, B), (64, 40, B)], sc, outer, zho, zlo, scratch=scratch, weight=10**8)


def middle_kernel(
    sc, own_all, rim_all, zhc_all, zlc_all, tmsg, outer_all, tmo,
    own1_all, tmc_all, zh2_all, zl2_all, own2_all, dmsg_all,
):
    lane = lanes()

    def views(step):
        own, rim = part(own_all, step, 8), part(rim_all, step, 8)
        zhc, zlc = part(zhc_all, step, 14), part(zlc_all, step, 14)

        def first_rows(t, b):
            near, _ = merged(own, rim, rim_all, t, b, sc)
            q = t * 5 + b
            return near + unpack3(zhc[q // 3], q % 3, 0) + unpack3(zlc[q // 3], q % 3, 24)

        return own, rim, first_rows

    def rims(step):
        _, _, first_rows = views(step)
        tmc = part(tmc_all, step - 8, 20)
        for t in range(0, 8, 2):
            for b in range(5):
                tmc[t // 2 * 5 + b] = jnp.where(lane < 64, first_rows(t, b), turn(first_rows(t + 1, b), 64))

    def cores(step):
        own, rim, first_rows = views(step)
        own1, own2 = part(own1_all, step, 8), part(own2_all, step, 8)
        zh2, zl2 = part(zh2_all, step, 8), part(zl2_all, step, 8)
        for t in range(8):
            for b in range(5):
                own1[t, 8 * b : 8 * b + 8, :] = first_rows(t, b)
        place = step - jnp.where(sc[3] == 0, 3, 0)
        valid = (place >= 0) & (place < 5)
        msg = part(tmsg, jnp.clip(place, 0, 4), 27)
        for t in range(8):
            ahead, behind = [], []
            for b in range(3):
                q = t * 3 + b
                near, far = merged(own, rim, rim_all, t, b + 5, sc)
                main = msg[q]
                moved = turn(msg[24 + q // 8], 88 - 16 * (q % 8))
                near = near + jnp.where(valid & (lane < 104), main, 0.0)
                far2 = jnp.where(lane >= 104, main, jnp.where(lane >= 88, moved, 0.0))
                far = far + jnp.where(valid, far2, 0.0)
                ahead.append(near)
                behind.append(far)
                own2[t, 8 * b : 8 * b + 8, :] = near
            zh2[t] = pack3(ahead, 64)
            zl2[t] = pack3(behind, 88)

    def outers(step):
        own, dmsg = part(outer_all, step, 8), part(dmsg_all, step, 20)
        for t in range(0, 8, 2):
            for b in range(5):
                even, odd = time_rows(sc, own, tmo, step, t, b), time_rows(sc, own, tmo, step, t + 1, b)
                dmsg[t // 2 * 5 + b] = jnp.where(lane < 64, even, turn(odd, 64))

    loop(8, 13, rims)
    loop(0, 8, outers)
    loop(0, 8, cores)


def middle(sc, *args):
    shapes = [(64, 40, B), (100, 8, B), (64, 8, B), (64, 8, B), (64, 24, B), (160, 8, B)]
    return call(middle_kernel, shapes, sc, *args)


def time_rows(sc, own, msg, step, t, b):
    place = step - jnp.where(sc[3] == 0, 3, 0)
    valid = (place >= 0) & (place < 5)
    both = msg[(jnp.clip(place, 0, 4) * 4 + t // 2) * 5 + b]
    both = both if t % 2 == 0 else turn(both, 64)
    return own[t, 8 * b : 8 * b + 8, :] + jnp.where(valid, both, 0.0)


def last_kernel(sc, own1_all, tmc, zh2_all, zl2_all, own2_all, dmsg_all, out_all):
    shift = jnp.where(sc[4] == 0, 0, 3)

    def body(step):
        own1, own2 = part(own1_all, step, 8), part(own2_all, step, 8)
        zh2, zl2 = part(zh2_all, step, 8), part(zl2_all, step, 8)
        dmsg, out = part(dmsg_all, step, 20), part(out_all, step, 8)
        for t in range(8):
            for b in range(8):
                if b < 5:
                    value = time_rows(sc, own1, tmc, step, t, b)
                else:
                    value = own2[t, 8 * (b - 5) : 8 * (b - 5) + 8, :]
                    value = value + unpack3(zh2[t], b - 5, 0) + unpack3(zl2[t], b - 5, 24)
                place = b - shift
                valid = (place >= 0) & (place < 5)
                other = dmsg[t // 2 * 5 + jnp.clip(place, 0, 4)]
                other = other if t % 2 == 0 else turn(other, 64)
                value = value + jnp.where(valid, other, 0.0)
                out[t, 8 * b : 8 * b + 8, :] = value[:, :64]

    loop(0, 8, body)


def last(sc, own1, tmc, zh2, zl2, own2, dmsg):
    return call(last_kernel, [(64, 64, 64)], sc, own1, tmc, zh2, zl2, own2, dmsg)[0]


def local(coef_fine, coef_coarse, kept, tile_offsets):
    tabs = [jnp.asarray(t) for t in tables()]
    n_tm, n_in, n_x = (lax.axis_size(a) for a in ("tm", "inline", "xline"))
    tm = lax.axis_index("tm").astype(jnp.int32)
    odd = (lax.axis_index("inline") & 1).astype(jnp.int32)
    sc = jnp.concatenate([tile_offsets.reshape(3), jnp.stack([tm, odd]), kept.reshape(6)])

    along = [(i, i + 1) for i in range(n_x - 1)]
    back = [(b, a) for a, b in along]
    inner = range(1, n_in - 1)
    along_o = [(i * n_x + a, i * n_x + b) for i in inner for a, b in along]
    back_o = [(b, a) for a, b in along_o]
    times = [(i, i ^ 1) for i in range(n_tm)]
    times_o = [(a * n_in + i, b * n_in + i) for i in inner for a, b in times]
    mates = [(i, i ^ 1) for i in range(n_in)]
    facing = [p for i in range(1, n_in - 1, 2) for p in ((i, i + 1), (i + 1, i))]

    rim, outer, zho, zlo, own = transform(sc, coef_fine, coef_coarse, tabs)
    rim = lax.ppermute(rim, "inline", mates)
    zho = lax.ppermute(zho, ("inline", "xline"), along_o)
    zlo = lax.ppermute(zlo, ("inline", "xline"), back_o)
    tmsg = pack_time(sc, own, rim)
    tmsg = lax.ppermute(tmsg, "tm", times)
    zhc, zlc = pack_xline(sc, own, rim)
    zhc = lax.ppermute(zhc, "xline", along)
    zlc = lax.ppermute(zlc, "xline", back)
    tmo, outer = outer_middle(sc, outer, zho, zlo)
    tmo = lax.ppermute(tmo, ("tm", "inline"), times_o)
    own1, tmc, zh2, zl2, own2, dmsg = middle(sc, own, rim, zhc, zlc, tmsg, outer, tmo)
    dmsg = lax.ppermute(dmsg, "inline", facing)
    tmc = lax.ppermute(tmc, "tm", times)
    zh2 = lax.ppermute(zh2, "xline", along)
    zl2 = lax.ppermute(zl2, "xline", back)
    return last(sc, own1, tmc, zh2, zl2, own2, dmsg)


def solution(mesh):
    in_specs = (
        P(None, "tm", "inline", "xline"),
        P(None, "tm", "inline", "xline"),
        P("tm", "inline", "xline", None),
        P("tm", "inline", "xline", None),
    )
    out_specs = P("tm", "inline", "xline")
    return jax.shard_map(local, mesh=mesh, in_specs=in_specs, out_specs=out_specs, check_vma=False)
```

```python
import math

import jax
import jax.numpy as jnp
import numpy as np
from jax import lax
from jax.experimental import pallas as pl
from jax.experimental.pallas import tpu as pltpu
from jax.sharding import PartitionSpec as P

B = 128
NW = 16
F32 = jnp.float32
BF16 = jnp.bfloat16
NTR = 104
VMEM = pltpu.VMEM
SMEM = pltpu.SMEM


def tables():
    f = np.where(np.arange(B) < B // 2, np.arange(B), np.arange(B) - B).astype(np.float64)
    theta = np.mod(np.arctan2(f[None, :], f[:, None]), np.pi)
    delta = np.pi / NW
    dist = np.mod(theta[None] - np.arange(NW)[:, None, None] * delta + np.pi / 2, np.pi) - np.pi / 2
    win = np.where(np.abs(dist) < delta, np.cos(0.5 * np.pi * dist / delta), 0.0)
    rows = np.concatenate([np.arange(0, 32), np.arange(96, 128)])
    radius = np.sqrt(np.arange(32.0)[:, None, None] ** 2 + f[rows][None, :, None] ** 2 + f[None, None, :] ** 2)
    ramp = np.clip((radius - 16.0) / 16.0, 0.0, 1.0)
    wf = np.where(ramp >= 1.0, 1.0, np.sin(0.5 * np.pi * ramp))
    wc = np.where(ramp >= 1.0, 0.0, np.cos(0.5 * np.pi * ramp))
    wf = wf.reshape(32, 2, 32, B).transpose(1, 0, 2, 3)
    wc = wc.reshape(32, 2, 32, B).transpose(1, 0, 2, 3)
    n = np.arange(B)
    p = np.where(n < 64, np.sin(np.pi * (n + 0.5) / B) ** 2, np.sin(np.pi * (B - n - 0.5) / B) ** 2)
    phase = 2 * np.pi * ((n[:, None] * n[None, :]) % B) / B
    c = np.cos(phase) * p[:, None] / math.sqrt(B)
    s = np.sin(phase) * p[:, None] / math.sqrt(B)
    e0 = np.stack([np.concatenate([c, -s], 1), np.concatenate([s, c], 1)])
    w2 = np.stack([np.concatenate([c, -s], 1).T, np.concatenate([s, c], 1).T])
    w1 = np.concatenate([c[:, :64], -s[:, :64]], 1)
    w1[:, 64] = c[:, 64]
    return [np.asarray(t, np.float32) for t in (win, wf, wc, e0, w2, w1)]


def split(x):
    hi = x.astype(BF16)
    return hi, (x - hi.astype(F32)).astype(BF16)


def dot(a, b):
    return lax.dot_general(a, b, (((1,), (0,)), ((), ())), preferred_element_type=F32)


def rows_of(table, offset):
    rolled = pltpu.roll(table, offset, 0)
    row = lax.broadcasted_iota(jnp.int32, (16, table.shape[1]), 0)
    shared = rolled[0:16]
    above = jnp.concatenate([rolled[104:128], jnp.where(row < offset, shared, 0.0)], axis=0)
    below = jnp.concatenate([jnp.where(row >= offset, shared, 0.0), rolled[16:40]], axis=0)
    return rolled[40:104], above, below


def doubled(table):
    hi, lo = split(table)
    hi, lo = hi.astype(F32), lo.astype(F32)
    top, bottom = jnp.concatenate([hi, hi], axis=1), jnp.concatenate([lo, jnp.zeros_like(lo)], axis=1)
    return jnp.concatenate([top, bottom], axis=0).astype(BF16)


def transform_kernel(
    sc, fine, coarse, win, wf, wc, e0t, w2t, w1t, rim_out, outer_out, zho, zlo, own_out,
    shi, slo, xhi, xlo, pq, ang, e0, w2, wm, gbuf,
):
    step = pl.program_id(0)
    o0, o1, o2, tm, odd = sc[0], sc[1], sc[2], sc[3], sc[4]

    @pl.when(step == 0)
    def _():
        total = win[sc[5]]
        for i in range(1, 6):
            total = total + win[sc[5 + i]]
        ang[...] = total
        parts = []
        for c in range(2):
            own, above, below = rows_of(e0t[c], o0)
            parts += [own, jnp.where(tm == 0, above, below)]
        hi, lo = split(jnp.concatenate(parts, axis=0))
        e0[:, 0:256] = hi
        e0[:, 256:512] = lo
        e0[:, 512:768] = hi
        for c in range(2):
            hi, lo = split(pltpu.roll(w2t[c], o2 + 88, 1))
            w2[c, 0:256] = jnp.concatenate([hi, lo], axis=1)
            w2[c, 256:512] = jnp.concatenate([hi, jnp.zeros_like(hi)], axis=1)
        own, above, below = rows_of(w1t[...], o1)
        mutual = jnp.where(odd == 0, above, below)
        outer = jnp.where(odd == 0, below, above)
        wm[...] = doubled(jnp.concatenate([mutual, outer, own], axis=0))

    @pl.when((step == 0) | (step == 3))
    def _():
        a = ang[pl.ds(pl.multiple_of(step * 32, 32), 32), :]
        row = lax.broadcasted_iota(jnp.int32, (32, B), 0)
        a = jnp.where((step == 3) & (row == 0), 1.0, a)

        def put(index, value):
            hi, lo = split(value)
            shi[index] = hi
            slo[index] = lo

        def plane(k0, j0, radial, coarse_w):
            for c in range(2):
                small = coarse[c, j0].astype(F32)
                small = jnp.concatenate([small, small], axis=1)
                put(c * B + k0, radial * fine[c, k0].astype(F32) + coarse_w * small)

        plane(0, 0, a * wf[0, 0], wc[0, 0])

        def low(q, _):
            radial = a * wf[0, q]
            coarse_w = wc[0, q]
            plane(q, q, radial, coarse_w)
            plane(B - q, 64 - q, radial, coarse_w)
            return 0

        lax.fori_loop(1, 32, low, 0, unroll=31)

        def high(i, _):
            for k0 in (32 + 2 * i, 33 + 2 * i):
                for c in range(2):
                    put(c * B + k0, a * fine[c, k0].astype(F32))
            return 0

        lax.fori_loop(0, 32, high, 0, unroll=4)
        for c in range(2):
            put(c * B + 96, a * fine[c, 96].astype(F32))
        xhi[pl.ds(step * 32, 32)] = jnp.swapaxes(shi[...], 0, 1)
        xlo[pl.ds(jnp.where(step == 0, 0, 32), 32)] = jnp.swapaxes(slo[...], 0, 1)

    @pl.when((step == 1) | (step == 2))
    def _():
        xhi[pl.ds(step * 32, 32)] = jnp.swapaxes(fine[...].reshape(256, 32, B), 0, 1)

    def along_xline(j):
        for which in range(2):
            out = dot(gbuf[which], w2[which])
            out = out[:, :B] + out[:, B:]
            for i in range(8):
                pq[which * 64 + j + i] = out[i * NTR : i * NTR + NTR]

    def hold(slot, even, odd_part):
        for which, pair in ((0, even), (1, odd_part)):
            wide = [jnp.concatenate([g[:NTR], g[NTR:]], axis=1) for g in pair]
            hi, lo = split(jnp.concatenate(wide, axis=0))
            gbuf[which, slot * 208 : slot * 208 + 208] = jnp.concatenate([hi, lo], axis=1)

    def first(k, kk, lo_pair):
        hi = jnp.concatenate([xhi[k], xhi[kk]], axis=1)
        if lo_pair is None:
            return dot(e0[:, 0:512], jnp.concatenate([hi, hi], axis=0))
        lo = jnp.concatenate(lo_pair, axis=1)
        return dot(e0[...], jnp.concatenate([hi, hi, lo], axis=0))

    def inner_pair(j):
        out = first(j, B - j, (xlo[j], xlo[64 - j]))
        return out[:, :B] + out[:, B:], out[:, :B] - out[:, B:]

    def outer_pair(j):
        out = first(j, B - j, None)
        a = out[:, :B] * ang[pl.ds(j, 1), :]
        b = out[:, B:] * ang[pl.ds(B - j, 1), :]
        return a + b, a - b

    @pl.when(step == 3)
    def _():
        out = first(0, 64, (xlo[0], jnp.zeros((256, B), BF16)))
        half = out[:, B:] * ang[64:65, :]
        even0 = out[:, :B]
        odd0 = jnp.concatenate([-half[NTR:], half[:NTR]], axis=0)
        even1, odd1 = inner_pair(1)
        hold(0, (even0, even1), (odd0, odd1))

        def group(pair, i, slots):
            for slot in slots:
                (ea, oa), (eb, ob) = pair(8 * i + 2 * slot), pair(8 * i + 2 * slot + 1)
                hold(slot, (ea, eb), (oa, ob))

        def eight(pair):
            def body(i, _):
                along_xline(8 * i - 8)
                group(pair, i, range(4))
                return 0

            return body

        group(inner_pair, 0, range(1, 4))
        lax.fori_loop(1, 4, eight(inner_pair), 0)
        lax.fori_loop(4, 8, eight(outer_pair), 0)
        along_xline(56)
        rim_out[13 * 8 : 14 * 8] = jnp.full((8, 40, B), o2.astype(F32), F32)

    @pl.when(step >= 4)
    def _():
        n0 = (step - 4) * 26
        ahead, behind = [], []
        for pair in range(13):
            x = jnp.concatenate([pq[:, n0 + 2 * pair, :], pq[:, n0 + 2 * pair + 1, :]], axis=1)
            hi, lo = split(x)
            rhs = jnp.concatenate([hi, lo], axis=0)
            out = dot(wm[...], rhs)
            out = out[:144] + out[144:]
            for half in range(2):
                part = out[:, half * B : half * B + B]
                rim_out[n0 + 2 * pair + half] = part[:40]
                outer_out[2 * pair + half] = part[40:80]
                own_out[2 * pair + half] = part[80:]
                for b in range(5):
                    near, far = two_sides(part[40 + 8 * b : 48 + 8 * b], o2)
                    ahead.append(near)
                    behind.append(far)
        pack_sides(ahead, behind, zho, zlo, sc)


def transform(scalars, fine, coarse, tabs):
    def edge(s):
        return jnp.minimum(s, 1)

    def late_step(s):
        return (jnp.maximum(s - 4, 0), 0, 0)

    whole = pl.BlockSpec(memory_space=VMEM)
    return pl.pallas_call(
        transform_kernel,
        grid=(8,),
        in_specs=[
            pl.BlockSpec(memory_space=SMEM),
            pl.BlockSpec((2, B, 32, B), lambda s: (0, 0, jnp.minimum(s, 3), 0)),
            pl.BlockSpec((2, 64, 32, 64), lambda s: (0, 0, edge(s), 0)),
            whole,
            pl.BlockSpec((1, 32, 32, B), lambda s: (edge(s), 0, 0, 0)),
            pl.BlockSpec((1, 32, 32, B), lambda s: (edge(s), 0, 0, 0)),
            whole,
            whole,
            whole,
        ],
        out_specs=[
            whole,
            pl.BlockSpec((26, 40, B), late_step),
            pl.BlockSpec((44, 8, B), late_step),
            pl.BlockSpec((44, 8, B), late_step),
            pl.BlockSpec((26, 64, B), late_step),
        ],
        out_shape=[
            jax.ShapeDtypeStruct((NTR + 8, 40, B), F32),
            jax.ShapeDtypeStruct((NTR, 40, B), F32),
            jax.ShapeDtypeStruct((4 * 44, 8, B), F32),
            jax.ShapeDtypeStruct((4 * 44, 8, B), F32),
            jax.ShapeDtypeStruct((NTR, 64, B), F32),
        ],
        scratch_shapes=[
            VMEM((256, 32, B), BF16),
            VMEM((256, 32, B), BF16),
            VMEM((B, 256, B), BF16),
            VMEM((64, 256, B), BF16),
            VMEM((B, NTR, B), F32),
            VMEM((B, B), F32),
            VMEM((208, 768), BF16),
            VMEM((2, 512, 256), BF16),
            VMEM((288, 256), BF16),
            VMEM((2, 832, 512), BF16),
        ],
        compiler_params=pltpu.CompilerParams(
            dimension_semantics=("arbitrary",), vmem_limit_bytes=63 * 2**20
        ),
        cost_estimate=pl.CostEstimate(flops=2 * 10**10, bytes_accessed=30 * 10**6, transcendentals=0),
    )(scalars, fine, coarse, *tabs)


def lanes():
    return lax.broadcasted_iota(jnp.int32, (8, B), 1)


def two_sides(value, offset):
    lane = lanes()
    return jnp.where(lane < 88 + offset, value, 0.0), jnp.where(lane >= 88 + offset, value, 0.0)


def turn(value, shift):
    shift = shift % B
    return value if shift == 0 else pltpu.roll(value, shift, 1)


def pack3(pieces, start):
    lane = lanes()
    out = turn(pieces[0], -start)
    for i in range(1, len(pieces)):
        out = jnp.where(lane < 40 * i, out, turn(pieces[i], 40 * i - start))
    return out


def unpack3(packed, place, start):
    lane = lanes()
    value = turn(packed, start - 40 * place)
    return jnp.where((lane >= start) & (lane < start + 40), value, 0.0)


def merged(own, rim, mate, t, b, sc):
    near, far = two_sides(own[t, 8 * b : 8 * b + 8, :], sc[2])
    place = b - jnp.where(sc[4] == 0, 3, 0)
    valid = (place >= 0) & (place < 5)
    place = jnp.clip(place, 0, 4)
    other = rim[t, pl.ds(pl.multiple_of(place * 8, 8), 8), :]
    other = jnp.where(valid, other, 0.0)
    upto = lanes().astype(F32) < 88.0 + mate[NTR, 0:8, :]
    return near + jnp.where(upto, other, 0.0), far + jnp.where(upto, 0.0, other)


def pack_sides(ahead, behind, first, second, sc):
    odd = sc[11] == 1
    for g in range((len(ahead) + 2) // 3):
        high = pack3(ahead[3 * g : 3 * g + 3], 64)
        low = pack3(behind[3 * g : 3 * g + 3], 88)
        first[g] = jnp.where(odd, low, high)
        second[g] = jnp.where(odd, high, low)


def unpack_sides(first, second, q, sc):
    odd = sc[11] == 1
    one, two = first[q // 3], second[q // 3]
    before, after = jnp.where(odd, one, two), jnp.where(odd, two, one)
    return unpack3(before, q % 3, 0) + unpack3(after, q % 3, 24)


def call(kernel, shapes, *args, scratch=(), weight=1000, token=False):
    specs = [pl.BlockSpec(memory_space=SMEM)] + [WHOLE] * (len(args) - 1)
    if token:
        specs[-1] = pl.BlockSpec(memory_space=pl.ANY)
    return pl.pallas_call(
        kernel,
        in_specs=specs,
        out_specs=[WHOLE] * len(shapes),
        out_shape=[jax.ShapeDtypeStruct(shape, F32) for shape in shapes],
        scratch_shapes=scratch,
        compiler_params=pltpu.CompilerParams(vmem_limit_bytes=20 * 2**20),
        cost_estimate=pl.CostEstimate(flops=1000, bytes_accessed=weight, transcendentals=0),
    )(*args)


WHOLE = pl.BlockSpec(memory_space=VMEM)


def part(ref, step, size):
    return ref.at[pl.ds(step * size, size)]


def loop(low, high, body):
    def run(i, _):
        body(i)
        return 0

    lax.fori_loop(low, high, run, 0)


def pack_time_kernel(sc, own_all, rim_all, tmsg):
    lane = lanes()

    def rims(step):
        own, rim, out = part(own_all, step, 8), part(rim_all, step, 8), part(tmsg, step - 8, 36)
        extra = None
        for t in range(8):
            for b in range(4):
                near, far = merged(own, rim, rim_all, t, b + 4, sc)
                q = t * 4 + b
                out[q] = jnp.where(lane < 104, near, far)
                moved = turn(far, 16 * (q % 8) - 88)
                extra = moved if q % 8 == 0 else jnp.where(lane < 16 * (q % 8), extra, moved)
                if q % 8 == 7:
                    out[32 + q // 8] = extra

    loop(8, 13, rims)


def pack_xline_kernel(sc, own_all, rim_all, token, zhc, zlc):
    def every(step):
        own, rim = part(own_all, step, 8), part(rim_all, step, 8)
        ahead, behind = [], []
        for t in range(8):
            for b in range(4):
                near, far = merged(own, rim, rim_all, t, b, sc)
                ahead.append(near)
                behind.append(far)
        pack_sides(ahead, behind, part(zhc, step, 11), part(zlc, step, 11), sc)

    loop(0, 13, every)


def outer_middle_kernel(sc, outer_all, zho_all, zlo_all, tmo, own, held):
    lane = lanes()

    def outers(step):
        zh, zl = part(zho_all, step, 44), part(zlo_all, step, 44)
        outer, out = part(outer_all, step, 26), part(held, step, 26)
        for t in range(26):
            for b in range(5):
                q = t * 5 + b
                out[t, 8 * b : 8 * b + 8, :] = outer[t, 8 * b : 8 * b + 8, :] + unpack_sides(zh, zl, q, sc)

    def outer_rims(p):
        for b in range(5):
            rows = slice(8 * b, 8 * b + 8)
            tmo[p * 5 + b] = jnp.where(lane < 64, held[64 + 2 * p, rows, :], turn(held[65 + 2 * p, rows, :], 64))

    loop(0, 4, outers)
    loop(0, 20, outer_rims)
    own[...] = held[0:64]


def pack_time(sc, own, rim):
    return call(pack_time_kernel, [(5 * 36, 8, B)], sc, own, rim)[0]


def pack_xline(sc, own, rim, token):
    return call(pack_xline_kernel, [(13 * 11, 8, B), (13 * 11, 8, B)], sc, own, rim, token, weight=10**8, token=True)


def outer_middle(sc, outer, zho, zlo):
    scratch = [VMEM((NTR, 40, B), F32)]
    return call(outer_middle_kernel, [(100, 8, B), (64, 40, B)], sc, outer, zho, zlo, scratch=scratch, weight=10**8)


def middle_xline_kernel(sc, own_all, rim_all, tmsg, zh2_all, zl2_all, own2_all):
    lane = lanes()

    def cores(step):
        own, rim, own2 = part(own_all, step, 8), part(rim_all, step, 8), part(own2_all, step, 8)
        place = step - jnp.where(sc[3] == 0, 3, 0)
        valid = (place >= 0) & (place < 5)
        msg = part(tmsg, jnp.clip(place, 0, 4), 36)
        ahead, behind = [], []
        for t in range(8):
            for b in range(4):
                q = t * 4 + b
                near, far = merged(own, rim, rim_all, t, b + 4, sc)
                main = msg[q]
                moved = turn(msg[32 + q // 8], 88 - 16 * (q % 8))
                near = near + jnp.where(valid & (lane < 104), main, 0.0)
                far2 = jnp.where(lane >= 104, main, jnp.where(lane >= 88, moved, 0.0))
                far = far + jnp.where(valid, far2, 0.0)
                ahead.append(near)
                behind.append(far)
                own2[t, 8 * b : 8 * b + 8, :] = near
        pack_sides(ahead, behind, part(zh2_all, step, 11), part(zl2_all, step, 11), sc)

    loop(0, 8, cores)


def middle_time_kernel(sc, own_all, rim_all, zhc_all, zlc_all, outer_all, tmo, token, own1_all, tmc_all, dmsg_all):
    lane = lanes()

    def views(step):
        own, rim = part(own_all, step, 8), part(rim_all, step, 8)
        zhc, zlc = part(zhc_all, step, 11), part(zlc_all, step, 11)

        def first_rows(t, b):
            near, _ = merged(own, rim, rim_all, t, b, sc)
            return near + unpack_sides(zhc, zlc, t * 4 + b, sc)

        return first_rows

    def rims(step):
        first_rows = views(step)
        tmc = part(tmc_all, step - 8, 16)
        for t in range(0, 8, 2):
            for b in range(4):
                tmc[t // 2 * 4 + b] = jnp.where(lane < 64, first_rows(t, b), turn(first_rows(t + 1, b), 64))

    def cores(step):
        first_rows = views(step)
        own1 = part(own1_all, step, 8)
        for t in range(8):
            for b in range(4):
                own1[t, 8 * b : 8 * b + 8, :] = first_rows(t, b)

    def outers(step):
        own, dmsg = part(outer_all, step, 8), part(dmsg_all, step, 20)
        for t in range(0, 8, 2):
            for b in range(5):
                even, odd = time_rows(sc, own, tmo, step, t, b, 5), time_rows(sc, own, tmo, step, t + 1, b, 5)
                dmsg[t // 2 * 5 + b] = jnp.where(lane < 64, even, turn(odd, 64))

    loop(8, 13, rims)
    loop(0, 8, outers)
    loop(0, 8, cores)


def middle_xline(sc, own, rim, tmsg):
    return call(middle_xline_kernel, [(88, 8, B), (88, 8, B), (64, 32, B)], sc, own, rim, tmsg, weight=10**8)


def middle_time(sc, *args):
    return call(middle_time_kernel, [(64, 32, B), (80, 8, B), (160, 8, B)], sc, *args, weight=10**8, token=True)


def time_rows(sc, own, msg, step, t, b, count):
    place = step - jnp.where(sc[3] == 0, 3, 0)
    valid = (place >= 0) & (place < 5)
    both = msg[(jnp.clip(place, 0, 4) * 4 + t // 2) * count + b]
    both = both if t % 2 == 0 else turn(both, 64)
    return own[t, 8 * b : 8 * b + 8, :] + jnp.where(valid, both, 0.0)


def last_kernel(sc, own1_all, tmc, zh2_all, zl2_all, own2_all, dmsg_all, out_all):
    shift = jnp.where(sc[4] == 0, 0, 3)

    def body(step):
        own1, own2 = part(own1_all, step, 8), part(own2_all, step, 8)
        zh2, zl2 = part(zh2_all, step, 11), part(zl2_all, step, 11)
        dmsg, out = part(dmsg_all, step, 20), part(out_all, step, 8)
        for t in range(8):
            for b in range(8):
                if b < 4:
                    value = time_rows(sc, own1, tmc, step, t, b, 4)
                else:
                    value = own2[t, 8 * (b - 4) : 8 * (b - 4) + 8, :]
                    value = value + unpack_sides(zh2, zl2, t * 4 + b - 4, sc)
                place = b - shift
                valid = (place >= 0) & (place < 5)
                other = dmsg[t // 2 * 5 + jnp.clip(place, 0, 4)]
                other = other if t % 2 == 0 else turn(other, 64)
                value = value + jnp.where(valid, other, 0.0)
                out[t, 8 * b : 8 * b + 8, :] = value[:, :64]

    loop(0, 8, body)


def last(sc, own1, tmc, zh2, zl2, own2, dmsg):
    return call(last_kernel, [(64, 64, 64)], sc, own1, tmc, zh2, zl2, own2, dmsg)[0]


def local(coef_fine, coef_coarse, kept, tile_offsets):
    tabs = [jnp.asarray(t) for t in tables()]
    n_tm, n_in, n_x = (lax.axis_size(a) for a in ("tm", "inline", "xline"))
    tm = lax.axis_index("tm").astype(jnp.int32)
    odd = (lax.axis_index("inline") & 1).astype(jnp.int32)
    xodd = (lax.axis_index("xline") & 1).astype(jnp.int32)
    sc = jnp.concatenate([tile_offsets.reshape(3), jnp.stack([tm, odd]), kept.reshape(6), xodd[None]])

    pairs = [(i, i ^ 1) for i in range(n_x)]
    between = [p for i in range(1, n_x - 1, 2) for p in ((i, i + 1), (i + 1, i))]
    inner = range(1, n_in - 1)
    pairs_o = [(i * n_x + a, i * n_x + b) for i in inner for a, b in pairs]
    between_o = [(i * n_x + a, i * n_x + b) for i in inner for a, b in between]
    times = [(i, i ^ 1) for i in range(n_tm)]
    times_o = [(a * n_in + i, b * n_in + i) for i in inner for a, b in times]
    mates = [(i, i ^ 1) for i in range(n_in)]
    facing = [p for i in range(1, n_in - 1, 2) for p in ((i, i + 1), (i + 1, i))]

    rim, outer, zho, zlo, own = transform(sc, coef_fine, coef_coarse, tabs)
    rim = lax.ppermute(rim, "inline", mates)
    zho = lax.ppermute(zho, ("inline", "xline"), pairs_o)
    zlo = lax.ppermute(zlo, ("inline", "xline"), between_o)
    packed = pack_time(sc, own, rim)
    tmsg = lax.ppermute(packed, "tm", times)
    zhc, zlc = pack_xline(sc, own, rim, packed)
    zhc = lax.ppermute(zhc, "xline", pairs)
    zlc = lax.ppermute(zlc, "xline", between)
    tmo, outer = outer_middle(sc, outer, zho, zlo)
    tmo = lax.ppermute(tmo, ("tm", "inline"), times_o)
    packed, zl2, own2 = middle_xline(sc, own, rim, tmsg)
    zh2 = lax.ppermute(packed, "xline", pairs)
    zl2 = lax.ppermute(zl2, "xline", between)
    own1, tmc, dmsg = middle_time(sc, own, rim, zhc, zlc, outer, tmo, packed)
    dmsg = lax.ppermute(dmsg, "inline", facing)
    tmc = lax.ppermute(tmc, "tm", times)
    return last(sc, own1, tmc, zh2, zl2, own2, dmsg)


def solution(mesh):
    in_specs = (
        P(None, "tm", "inline", "xline"),
        P(None, "tm", "inline", "xline"),
        P("tm", "inline", "xline", None),
        P("tm", "inline", "xline", None),
    )
    out_specs = P("tm", "inline", "xline")
    return jax.shard_map(local, mesh=mesh, in_specs=in_specs, out_specs=out_specs, check_vma=False)
```

```python
import math

import jax
import jax.numpy as jnp
import numpy as np
from jax import lax
from jax.experimental import pallas as pl
from jax.experimental.pallas import tpu as pltpu
from jax.sharding import PartitionSpec as P

B = 128
NW = 16
F32 = jnp.float32
BF16 = jnp.bfloat16
NTR = 104
VMEM = pltpu.VMEM
SMEM = pltpu.SMEM


def tables():
    f = np.where(np.arange(B) < B // 2, np.arange(B), np.arange(B) - B).astype(np.float64)
    theta = np.mod(np.arctan2(f[None, :], f[:, None]), np.pi)
    delta = np.pi / NW
    dist = np.mod(theta[None] - np.arange(NW)[:, None, None] * delta + np.pi / 2, np.pi) - np.pi / 2
    win = np.where(np.abs(dist) < delta, np.cos(0.5 * np.pi * dist / delta), 0.0)
    rows = np.concatenate([np.arange(0, 32), np.arange(96, 128)])
    radius = np.sqrt(np.arange(32.0)[:, None, None] ** 2 + f[rows][None, :, None] ** 2 + f[None, None, :] ** 2)
    ramp = np.clip((radius - 16.0) / 16.0, 0.0, 1.0)
    wf = np.where(ramp >= 1.0, 1.0, np.sin(0.5 * np.pi * ramp))
    wc = np.where(ramp >= 1.0, 0.0, np.cos(0.5 * np.pi * ramp))
    wf = wf.reshape(32, 2, 32, B).transpose(1, 0, 2, 3)
    wc = wc.reshape(32, 2, 32, B).transpose(1, 0, 2, 3)
    n = np.arange(B)
    p = np.where(n < 64, np.sin(np.pi * (n + 0.5) / B) ** 2, np.sin(np.pi * (B - n - 0.5) / B) ** 2)
    phase = 2 * np.pi * ((n[:, None] * n[None, :]) % B) / B
    c = np.cos(phase) * p[:, None] / math.sqrt(B)
    s = np.sin(phase) * p[:, None] / math.sqrt(B)
    e0 = np.stack([np.concatenate([c, -s], 1), np.concatenate([s, c], 1)])
    w2 = np.stack([np.concatenate([c, -s], 1).T, np.concatenate([s, c], 1).T])
    w1 = np.concatenate([c[:, :64], -s[:, :64]], 1)
    w1[:, 64] = c[:, 64]
    return [np.asarray(t, np.float32) for t in (win, wf, wc, e0, w2, w1)]


def split(x):
    hi = x.astype(BF16)
    return hi, (x - hi.astype(F32)).astype(BF16)


def dot(a, b):
    return lax.dot_general(a, b, (((1,), (0,)), ((), ())), preferred_element_type=F32)


def rows_of(table, offset):
    rolled = pltpu.roll(table, offset, 0)
    row = lax.broadcasted_iota(jnp.int32, (16, table.shape[1]), 0)
    shared = rolled[0:16]
    above = jnp.concatenate([rolled[104:128], jnp.where(row < offset, shared, 0.0)], axis=0)
    below = jnp.concatenate([jnp.where(row >= offset, shared, 0.0), rolled[16:40]], axis=0)
    return rolled[40:104], above, below


def doubled(table):
    hi, lo = split(table)
    hi, lo = hi.astype(F32), lo.astype(F32)
    top, bottom = jnp.concatenate([hi, hi], axis=1), jnp.concatenate([lo, jnp.zeros_like(lo)], axis=1)
    return jnp.concatenate([top, bottom], axis=0).astype(BF16)


def transform_kernel(
    sc, fine, coarse, win, wf, wc, e0t, w2t, w1t, rim_out, outer_out, zho, zlo, own_out,
    shi, slo, xhi, xlo, pq, ang, e0, w2, wm, gbuf,
):
    step = pl.program_id(0)
    o0, o1, o2, tm, odd = sc[0], sc[1], sc[2], sc[3], sc[4]

    @pl.when(step == 0)
    def _():
        total = win[sc[5]]
        for i in range(1, 6):
            total = total + win[sc[5 + i]]
        ang[...] = total
        parts = []
        for c in range(2):
            own, above, below = rows_of(e0t[c], o0)
            parts += [own, jnp.where(tm == 0, above, below)]
        hi, lo = split(jnp.concatenate(parts, axis=0))
        e0[:, 0:256] = hi
        e0[:, 256:512] = lo
        e0[:, 512:768] = hi
        for c in range(2):
            hi, lo = split(pltpu.roll(w2t[c], o2 + 88, 1))
            w2[c, 0:256] = jnp.concatenate([hi, lo], axis=1)
            w2[c, 256:512] = jnp.concatenate([hi, jnp.zeros_like(hi)], axis=1)
        own, above, below = rows_of(w1t[...], o1)
        mutual = jnp.where(odd == 0, above, below)
        outer = jnp.where(odd == 0, below, above)
        wm[...] = doubled(jnp.concatenate([mutual, outer, own], axis=0))

    @pl.when((step == 0) | (step == 3))
    def _():
        a = ang[pl.ds(pl.multiple_of(step * 32, 32), 32), :]
        row = lax.broadcasted_iota(jnp.int32, (32, B), 0)
        a = jnp.where((step == 3) & (row == 0), 1.0, a)

        def put(index, value):
            hi, lo = split(value)
            shi[index] = hi
            slo[index] = lo

        def plane(k0, j0, radial, coarse_w):
            for c in range(2):
                small = coarse[c, j0].astype(F32)
                small = jnp.concatenate([small, small], axis=1)
                put(c * B + k0, radial * fine[c, k0].astype(F32) + coarse_w * small)

        plane(0, 0, a * wf[0, 0], wc[0, 0])

        def low(q, _):
            radial = a * wf[0, q]
            coarse_w = wc[0, q]
            plane(q, q, radial, coarse_w)
            plane(B - q, 64 - q, radial, coarse_w)
            return 0

        lax.fori_loop(1, 32, low, 0, unroll=31)

        def high(i, _):
            for k0 in (32 + 2 * i, 33 + 2 * i):
                for c in range(2):
                    put(c * B + k0, a * fine[c, k0].astype(F32))
            return 0

        lax.fori_loop(0, 32, high, 0, unroll=4)
        for c in range(2):
            put(c * B + 96, a * fine[c, 96].astype(F32))
        for c in range(0, 256, 16):
            xhi[pl.ds(step * 32, 32), c : c + 16] = jnp.swapaxes(shi[c : c + 16], 0, 1)
            xlo[pl.ds(jnp.where(step == 0, 0, 32), 32), c : c + 16] = jnp.swapaxes(slo[c : c + 16], 0, 1)

    @pl.when((step == 1) | (step == 2))
    def _():
        for c in range(2):
            for k in range(0, B, 64):
                xhi[pl.ds(step * 32, 32), c * B + k : c * B + k + 64] = jnp.swapaxes(fine[c, k : k + 64], 0, 1)

    def along_xline(j):
        for which in range(2):
            out = dot(gbuf[which], w2[which])
            out = out[:, :B] + out[:, B:]
            for i in range(8):
                pq[which * 64 + j + i] = out[i * NTR : i * NTR + NTR]

    def hold(slot, even, odd_part):
        for which, pair in ((0, even), (1, odd_part)):
            wide = [jnp.concatenate([g[:NTR], g[NTR:]], axis=1) for g in pair]
            hi, lo = split(jnp.concatenate(wide, axis=0))
            gbuf[which, slot * 208 : slot * 208 + 208] = jnp.concatenate([hi, lo], axis=1)

    def first(k, kk, lo_pair):
        hi = jnp.concatenate([xhi[k], xhi[kk]], axis=1)
        if lo_pair is None:
            return dot(e0[:, 0:512], jnp.concatenate([hi, hi], axis=0))
        lo = jnp.concatenate(lo_pair, axis=1)
        return dot(e0[...], jnp.concatenate([hi, hi, lo], axis=0))

    def inner_pair(j):
        out = first(j, B - j, (xlo[j], xlo[64 - j]))
        return out[:, :B] + out[:, B:], out[:, :B] - out[:, B:]

    def outer_pair(j):
        out = first(j, B - j, None)
        a = out[:, :B] * ang[pl.ds(j, 1), :]
        b = out[:, B:] * ang[pl.ds(B - j, 1), :]
        return a + b, a - b

    @pl.when(step == 3)
    def _():
        out = first(0, 64, (xlo[0], jnp.zeros((256, B), BF16)))
        half = out[:, B:] * ang[64:65, :]
        even0 = out[:, :B]
        odd0 = jnp.concatenate([-half[NTR:], half[:NTR]], axis=0)
        even1, odd1 = inner_pair(1)
        hold(0, (even0, even1), (odd0, odd1))

        def group(pair, i, slots):
            for slot in slots:
                (ea, oa), (eb, ob) = pair(8 * i + 2 * slot), pair(8 * i + 2 * slot + 1)
                hold(slot, (ea, eb), (oa, ob))

        def eight(pair):
            def body(i, _):
                along_xline(8 * i - 8)
                group(pair, i, range(4))
                return 0

            return body

        group(inner_pair, 0, range(1, 4))
        lax.fori_loop(1, 4, eight(inner_pair), 0)
        lax.fori_loop(4, 8, eight(outer_pair), 0)
        along_xline(56)
        rim_out[13 * 8 : 14 * 8] = jnp.full((8, 40, B), o2.astype(F32), F32)

    @pl.when(step >= 4)
    def _():
        n0 = (step - 4) * 26
        ahead, behind = [], []
        for pair in range(13):
            x = jnp.concatenate([pq[:, n0 + 2 * pair, :], pq[:, n0 + 2 * pair + 1, :]], axis=1)
            hi, lo = split(x)
            rhs = jnp.concatenate([hi, lo], axis=0)
            out = dot(wm[...], rhs)
            out = out[:144] + out[144:]
            for half in range(2):
                part = out[:, half * B : half * B + B]
                rim_out[n0 + 2 * pair + half] = part[:40]
                outer_out[2 * pair + half] = part[40:80]
                own_out[2 * pair + half] = part[80:]
                for b in range(5):
                    near, far = two_sides(part[40 + 8 * b : 48 + 8 * b], o2)
                    ahead.append(near)
                    behind.append(far)
        pack_sides(ahead, behind, zho, zlo, sc)


def transform(scalars, fine, coarse, tabs):
    def edge(s):
        return jnp.minimum(s, 1)

    def late_step(s):
        return (jnp.maximum(s - 4, 0), 0, 0)

    whole = pl.BlockSpec(memory_space=VMEM)
    return pl.pallas_call(
        transform_kernel,
        grid=(8,),
        in_specs=[
            pl.BlockSpec(memory_space=SMEM),
            pl.BlockSpec((2, B, 32, B), lambda s: (0, 0, jnp.minimum(s, 3), 0)),
            pl.BlockSpec((2, 64, 32, 64), lambda s: (0, 0, edge(s), 0)),
            whole,
            pl.BlockSpec((1, 32, 32, B), lambda s: (edge(s), 0, 0, 0)),
            pl.BlockSpec((1, 32, 32, B), lambda s: (edge(s), 0, 0, 0)),
            whole,
            whole,
            whole,
        ],
        out_specs=[
            whole,
            pl.BlockSpec((26, 40, B), late_step),
            pl.BlockSpec((44, 8, B), late_step),
            pl.BlockSpec((44, 8, B), late_step),
            pl.BlockSpec((26, 64, B), late_step),
        ],
        out_shape=[
            jax.ShapeDtypeStruct((NTR + 8, 40, B), F32),
            jax.ShapeDtypeStruct((NTR, 40, B), F32),
            jax.ShapeDtypeStruct((4 * 44, 8, B), F32),
            jax.ShapeDtypeStruct((4 * 44, 8, B), F32),
            jax.ShapeDtypeStruct((NTR, 64, B), F32),
        ],
        scratch_shapes=[
            VMEM((256, 32, B), BF16),
            VMEM((256, 32, B), BF16),
            VMEM((B, 256, B), BF16),
            VMEM((64, 256, B), BF16),
            VMEM((B, NTR, B), F32),
            VMEM((B, B), F32),
            VMEM((208, 768), BF16),
            VMEM((2, 512, 256), BF16),
            VMEM((288, 256), BF16),
            VMEM((2, 832, 512), BF16),
        ],
        compiler_params=pltpu.CompilerParams(
            dimension_semantics=("arbitrary",), vmem_limit_bytes=63 * 2**20
        ),
        cost_estimate=pl.CostEstimate(flops=2 * 10**10, bytes_accessed=30 * 10**6, transcendentals=0),
    )(scalars, fine, coarse, *tabs)


def lanes():
    return lax.broadcasted_iota(jnp.int32, (8, B), 1)


def two_sides(value, offset):
    lane = lanes()
    return jnp.where(lane < 88 + offset, value, 0.0), jnp.where(lane >= 88 + offset, value, 0.0)


def turn(value, shift):
    shift = shift % B
    return value if shift == 0 else pltpu.roll(value, shift, 1)


def pack3(pieces, start):
    lane = lanes()
    out = turn(pieces[0], -start)
    for i in range(1, len(pieces)):
        out = jnp.where(lane < 40 * i, out, turn(pieces[i], 40 * i - start))
    return out


def unpack3(packed, place, start):
    lane = lanes()
    value = turn(packed, start - 40 * place)
    return jnp.where((lane >= start) & (lane < start + 40), value, 0.0)


def merged(own, rim, mate, t, b, sc):
    near, far = two_sides(own[t, 8 * b : 8 * b + 8, :], sc[2])
    place = b - jnp.where(sc[4] == 0, 3, 0)
    valid = (place >= 0) & (place < 5)
    place = jnp.clip(place, 0, 4)
    other = rim[t, pl.ds(pl.multiple_of(place * 8, 8), 8), :]
    other = jnp.where(valid, other, 0.0)
    upto = lanes().astype(F32) < 88.0 + mate[NTR, 0:8, :]
    return near + jnp.where(upto, other, 0.0), far + jnp.where(upto, 0.0, other)


def pack_sides(ahead, behind, first, second, sc):
    odd = sc[11] == 1
    for g in range((len(ahead) + 2) // 3):
        high = pack3(ahead[3 * g : 3 * g + 3], 64)
        low = pack3(behind[3 * g : 3 * g + 3], 88)
        first[g] = jnp.where(odd, low, high)
        second[g] = jnp.where(odd, high, low)


def unpack_sides(first, second, q, sc):
    odd = sc[11] == 1
    one, two = first[q // 3], second[q // 3]
    before, after = jnp.where(odd, one, two), jnp.where(odd, two, one)
    return unpack3(before, q % 3, 0) + unpack3(after, q % 3, 24)


def call(kernel, shapes, *args, scratch=(), weight=1000, token=False):
    specs = [pl.BlockSpec(memory_space=SMEM)] + [WHOLE] * (len(args) - 1)
    if token:
        specs[-1] = pl.BlockSpec(memory_space=pl.ANY)
    return pl.pallas_call(
        kernel,
        in_specs=specs,
        out_specs=[WHOLE] * len(shapes),
        out_shape=[jax.ShapeDtypeStruct(shape, F32) for shape in shapes],
        scratch_shapes=scratch,
        compiler_params=pltpu.CompilerParams(vmem_limit_bytes=20 * 2**20),
        cost_estimate=pl.CostEstimate(flops=1000, bytes_accessed=weight, transcendentals=0),
    )(*args)


WHOLE = pl.BlockSpec(memory_space=VMEM)


def part(ref, step, size):
    return ref.at[pl.ds(step * size, size)]


def loop(low, high, body):
    def run(i, _):
        body(i)
        return 0

    lax.fori_loop(low, high, run, 0)


def pack_time_kernel(sc, own_all, rim_all, tmsg):
    lane = lanes()

    def rims(step):
        own, rim, out = part(own_all, step, 8), part(rim_all, step, 8), part(tmsg, step - 8, 36)
        extra = None
        for t in range(8):
            for b in range(4):
                near, far = merged(own, rim, rim_all, t, b + 4, sc)
                q = t * 4 + b
                out[q] = jnp.where(lane < 104, near, far)
                moved = turn(far, 16 * (q % 8) - 88)
                extra = moved if q % 8 == 0 else jnp.where(lane < 16 * (q % 8), extra, moved)
                if q % 8 == 7:
                    out[32 + q // 8] = extra

    loop(8, 13, rims)


def pack_xline_kernel(sc, own_all, rim_all, token, zhc, zlc):
    def every(step):
        own, rim = part(own_all, step, 8), part(rim_all, step, 8)
        ahead, behind = [], []
        for t in range(8):
            for b in range(4):
                near, far = merged(own, rim, rim_all, t, b, sc)
                ahead.append(near)
                behind.append(far)
        pack_sides(ahead, behind, part(zhc, step, 11), part(zlc, step, 11), sc)

    loop(0, 13, every)


def outer_middle_kernel(sc, outer_all, zho_all, zlo_all, tmo, own, held):
    lane = lanes()

    def outers(step):
        zh, zl = part(zho_all, step, 44), part(zlo_all, step, 44)
        outer, out = part(outer_all, step, 26), part(held, step, 26)
        for t in range(26):
            for b in range(5):
                q = t * 5 + b
                out[t, 8 * b : 8 * b + 8, :] = outer[t, 8 * b : 8 * b + 8, :] + unpack_sides(zh, zl, q, sc)

    def outer_rims(p):
        for b in range(5):
            rows = slice(8 * b, 8 * b + 8)
            tmo[p * 5 + b] = jnp.where(lane < 64, held[64 + 2 * p, rows, :], turn(held[65 + 2 * p, rows, :], 64))

    loop(0, 4, outers)
    loop(0, 20, outer_rims)
    own[...] = held[0:64]


def pack_time(sc, own, rim):
    return call(pack_time_kernel, [(5 * 36, 8, B)], sc, own, rim)[0]


def pack_xline(sc, own, rim, token):
    return call(pack_xline_kernel, [(13 * 11, 8, B), (13 * 11, 8, B)], sc, own, rim, token, weight=10**8, token=True)


def outer_middle(sc, outer, zho, zlo):
    scratch = [VMEM((NTR, 40, B), F32)]
    return call(outer_middle_kernel, [(100, 8, B), (64, 40, B)], sc, outer, zho, zlo, scratch=scratch, weight=10**8)


def middle_xline_kernel(sc, own_all, rim_all, tmsg, zh2_all, zl2_all, own2_all):
    lane = lanes()

    def cores(step):
        own, rim, own2 = part(own_all, step, 8), part(rim_all, step, 8), part(own2_all, step, 8)
        place = step - jnp.where(sc[3] == 0, 3, 0)
        valid = (place >= 0) & (place < 5)
        msg = part(tmsg, jnp.clip(place, 0, 4), 36)
        ahead, behind = [], []
        for t in range(8):
            for b in range(4):
                q = t * 4 + b
                near, far = merged(own, rim, rim_all, t, b + 4, sc)
                main = msg[q]
                moved = turn(msg[32 + q // 8], 88 - 16 * (q % 8))
                near = near + jnp.where(valid & (lane < 104), main, 0.0)
                far2 = jnp.where(lane >= 104, main, jnp.where(lane >= 88, moved, 0.0))
                far = far + jnp.where(valid, far2, 0.0)
                ahead.append(near)
                behind.append(far)
                own2[t, 8 * b : 8 * b + 8, :] = near
        pack_sides(ahead, behind, part(zh2_all, step, 11), part(zl2_all, step, 11), sc)

    loop(0, 8, cores)


def middle_time_kernel(sc, own_all, rim_all, zhc_all, zlc_all, outer_all, tmo, token, own1_all, tmc_all, dmsg_all):
    lane = lanes()

    def views(step):
        own, rim = part(own_all, step, 8), part(rim_all, step, 8)
        zhc, zlc = part(zhc_all, step, 11), part(zlc_all, step, 11)

        def first_rows(t, b):
            near, _ = merged(own, rim, rim_all, t, b, sc)
            return near + unpack_sides(zhc, zlc, t * 4 + b, sc)

        return first_rows

    def rims(step):
        first_rows = views(step)
        tmc = part(tmc_all, step - 8, 16)
        for t in range(0, 8, 2):
            for b in range(4):
                tmc[t // 2 * 4 + b] = jnp.where(lane < 64, first_rows(t, b), turn(first_rows(t + 1, b), 64))

    def cores(step):
        first_rows = views(step)
        own1 = part(own1_all, step, 8)
        for t in range(8):
            for b in range(4):
                own1[t, 8 * b : 8 * b + 8, :] = first_rows(t, b)

    def outers(step):
        own, dmsg = part(outer_all, step, 8), part(dmsg_all, step, 20)
        for t in range(0, 8, 2):
            for b in range(5):
                even, odd = time_rows(sc, own, tmo, step, t, b, 5), time_rows(sc, own, tmo, step, t + 1, b, 5)
                dmsg[t // 2 * 5 + b] = jnp.where(lane < 64, even, turn(odd, 64))

    loop(8, 13, rims)
    loop(0, 8, outers)
    loop(0, 8, cores)


def middle_xline(sc, own, rim, tmsg):
    return call(middle_xline_kernel, [(88, 8, B), (88, 8, B), (64, 32, B)], sc, own, rim, tmsg, weight=10**8)


def middle_time(sc, *args):
    return call(middle_time_kernel, [(64, 32, B), (80, 8, B), (160, 8, B)], sc, *args, weight=10**8, token=True)


def time_rows(sc, own, msg, step, t, b, count):
    place = step - jnp.where(sc[3] == 0, 3, 0)
    valid = (place >= 0) & (place < 5)
    both = msg[(jnp.clip(place, 0, 4) * 4 + t // 2) * count + b]
    both = both if t % 2 == 0 else turn(both, 64)
    return own[t, 8 * b : 8 * b + 8, :] + jnp.where(valid, both, 0.0)


def last_kernel(sc, own1_all, tmc, zh2_all, zl2_all, own2_all, dmsg_all, out_all):
    shift = jnp.where(sc[4] == 0, 0, 3)

    def body(step):
        own1, own2 = part(own1_all, step, 8), part(own2_all, step, 8)
        zh2, zl2 = part(zh2_all, step, 11), part(zl2_all, step, 11)
        dmsg, out = part(dmsg_all, step, 20), part(out_all, step, 8)
        for t in range(8):
            for b in range(8):
                if b < 4:
                    value = time_rows(sc, own1, tmc, step, t, b, 4)
                else:
                    value = own2[t, 8 * (b - 4) : 8 * (b - 4) + 8, :]
                    value = value + unpack_sides(zh2, zl2, t * 4 + b - 4, sc)
                place = b - shift
                valid = (place >= 0) & (place < 5)
                other = dmsg[t // 2 * 5 + jnp.clip(place, 0, 4)]
                other = other if t % 2 == 0 else turn(other, 64)
                value = value + jnp.where(valid, other, 0.0)
                out[t, 8 * b : 8 * b + 8, :] = value[:, :64]

    loop(0, 8, body)


def last(sc, own1, tmc, zh2, zl2, own2, dmsg):
    return call(last_kernel, [(64, 64, 64)], sc, own1, tmc, zh2, zl2, own2, dmsg)[0]


def local(coef_fine, coef_coarse, kept, tile_offsets):
    tabs = [jnp.asarray(t) for t in tables()]
    n_tm, n_in, n_x = (lax.axis_size(a) for a in ("tm", "inline", "xline"))
    tm = lax.axis_index("tm").astype(jnp.int32)
    odd = (lax.axis_index("inline") & 1).astype(jnp.int32)
    xodd = (lax.axis_index("xline") & 1).astype(jnp.int32)
    sc = jnp.concatenate([tile_offsets.reshape(3), jnp.stack([tm, odd]), kept.reshape(6), xodd[None]])

    pairs = [(i, i ^ 1) for i in range(n_x)]
    between = [p for i in range(1, n_x - 1, 2) for p in ((i, i + 1), (i + 1, i))]
    inner = range(1, n_in - 1)
    pairs_o = [(i * n_x + a, i * n_x + b) for i in inner for a, b in pairs]
    between_o = [(i * n_x + a, i * n_x + b) for i in inner for a, b in between]
    times = [(i, i ^ 1) for i in range(n_tm)]
    times_o = [(a * n_in + i, b * n_in + i) for i in inner for a, b in times]
    mates = [(i, i ^ 1) for i in range(n_in)]
    facing = [p for i in range(1, n_in - 1, 2) for p in ((i, i + 1), (i + 1, i))]

    rim, outer, zho, zlo, own = transform(sc, coef_fine, coef_coarse, tabs)
    rim = lax.ppermute(rim, "inline", mates)
    zho = lax.ppermute(zho, ("inline", "xline"), pairs_o)
    zlo = lax.ppermute(zlo, ("inline", "xline"), between_o)
    packed = pack_time(sc, own, rim)
    tmsg = lax.ppermute(packed, "tm", times)
    zhc, zlc = pack_xline(sc, own, rim, packed)
    zhc = lax.ppermute(zhc, "xline", pairs)
    zlc = lax.ppermute(zlc, "xline", between)
    tmo, outer = outer_middle(sc, outer, zho, zlo)
    tmo = lax.ppermute(tmo, ("tm", "inline"), times_o)
    packed, zl2, own2 = middle_xline(sc, own, rim, tmsg)
    zh2 = lax.ppermute(packed, "xline", pairs)
    zl2 = lax.ppermute(zl2, "xline", between)
    own1, tmc, dmsg = middle_time(sc, own, rim, zhc, zlc, outer, tmo, packed)
    dmsg = lax.ppermute(dmsg, "inline", facing)
    tmc = lax.ppermute(tmc, "tm", times)
    return last(sc, own1, tmc, zh2, zl2, own2, dmsg)


def solution(mesh):
    in_specs = (
        P(None, "tm", "inline", "xline"),
        P(None, "tm", "inline", "xline"),
        P("tm", "inline", "xline", None),
        P("tm", "inline", "xline", None),
    )
    out_specs = P("tm", "inline", "xline")
    return jax.shard_map(local, mesh=mesh, in_specs=in_specs, out_specs=out_specs, check_vma=False)
```
